512 devices in a mesh: ta: 4 (over x), ha: 4 (over y_hi), wa: 32 (over z, y_lo, core).
Axes of the slice: x: 4, y: 8 (y_hi: 4, y_lo: 2; y = y_hi * 2 + y_lo), z: 8, core: 2. Of those that a mesh axis runs over, the one named last changes fastest.
Arguments:
- teacher_in: bfloat16 [8, 128, 256, 192], P('ta', 'ha', 'wa'), may hold values from -3 to 3
- teacher_weights: bfloat16 [1, 2, 3, 3, 3, 192, 192], replicated, may hold values from -0.4375 to 0.4375
- student_in: bfloat16 [8, 128, 256, 128], P('ta', ('ha', 'wa')), may hold values from -6 to 6
- depth_weights: float32 [4, 3, 3, 3, 128], replicated, may hold values from -1.25 to 1.25
- point_weights: bfloat16 [4, 128, 128], replicated, may hold values from -0.5 to 0.5
- project_weight: bfloat16 [128, 192], replicated, may hold values from -0.5 to 0.5
Outputs:
- voxel_grad: bfloat16 [8, 128, 256, 128], P('ta', ('ha', 'wa'))
The draws below stay inside these ranges and needn't reach their ends.
All inputs are finite; a program needn't handle non-finite values.
Results may differ from the reference program's by a relative error of at most 0.01.
Values may be sent and summed in bfloat16 or wider, within the bound.
A program may use at most 128 MiB of HBM per device.

```python
import jax
import jax.numpy as jnp
from jax import lax

CT = 192
CS = 128
BLOCKS = 1
LAYERS = 4
NT = 8
NH = 128
NW = 256


def shard_levels(stream_key, dims, pieces, low, largest):
    def one(dim, shards_of):
        draws = jax.random.uniform(jax.random.fold_in(jax.random.fold_in(stream_key, 6), dim), (shards_of,), jnp.float32, low / len(pieces), largest / len(pieces))
        return jnp.repeat(jnp.exp(draws), dims[dim] // shards_of).reshape((-1,) + (1,) * (len(dims) - dim - 1))

    level = one(*pieces[0])
    for cut in pieces[1:]:
        level = level * one(*cut)
    return level


def noise(own_key, shape, width, limit, shards=(), kind=jnp.bfloat16):
    factor_of = shard_levels(own_key, shape, shards, -0.22, 0.18) if shards else 1.0
    entries = jax.random.normal(own_key, shape, jnp.float32) * width * factor_of
    return jnp.minimum(jnp.maximum(entries, -limit), limit).astype(kind)


def setup_inputs(seed: int = 0) -> dict:
    keys = jax.random.split(jax.random.key(seed), 7)
    return {
        "teacher_in": noise(keys[0], (NT, NH, NW, CT), 0.5, 3.0, ((0, 4), (1, 4), (2, 32))),
        "teacher_weights": noise(keys[1], (BLOCKS, 2, 3, 3, 3, CT, CT), CT ** -0.5, 0.4375),
        "student_in": noise(keys[2], (NT, NH, NW, CS), 1.0, 6.0, ((0, 4), (1, 128))),
        "depth_weights": noise(keys[3], (LAYERS, 3, 3, 3, CS), 27 ** -0.5, 1.25, (), jnp.float32),
        "point_weights": noise(keys[4], (LAYERS, CS, CS), CS ** -0.5, 0.5),
        "project_weight": noise(keys[5], (CS, CT), CS ** -0.5, 0.5),
    }


def root_norm(field):
    return field * lax.rsqrt(lax.optimization_barrier(jnp.mean(field * field, axis=-1, keepdims=True)) + 1e-06)

def silu_slope(field):
    sigmoid_value = jax.nn.sigmoid(field)
    return sigmoid_value * (1.0 + field * (1.0 - sigmoid_value))

def causal_pad(field):
    return jnp.pad(field, ((2, 0), (1, 1), (1, 1), (0, 0)))

def future_pad(field):
    return jnp.pad(field, ((0, 2), (1, 1), (1, 1), (0, 0)))

def dense_conv(extended, kernel):
    frame_count = extended.shape[0] - 2
    row_count = extended.shape[1] - 2
    col_count = extended.shape[2] - 2
    channels = kernel.shape[-1]
    summed = jnp.zeros((frame_count * row_count * col_count, channels), jnp.float32)
    for step_t in range(3):
        for step_h in range(3):
            for step_w in range(3):
                tap_slice = extended[step_t:step_t + frame_count, step_h:step_h + row_count, step_w:step_w + col_count]
                summed = summed + jnp.dot(tap_slice.reshape(-1, tap_slice.shape[-1]), kernel[step_t, step_h, step_w], preferred_element_type=jnp.float32)
    return summed.reshape(frame_count, row_count, col_count, channels)

def depthwise(extended, kernel):
    frame_count = extended.shape[0] - 2
    row_count = extended.shape[1] - 2
    col_count = extended.shape[2] - 2
    summed = jnp.zeros((frame_count, row_count, col_count, kernel.shape[-1]), jnp.float32)
    for step_t in range(3):
        for step_h in range(3):
            for step_w in range(3):
                tap_slice = extended[step_t:step_t + frame_count, step_h:step_h + row_count, step_w:step_w + col_count]
                summed = summed + tap_slice.astype(jnp.float32) * kernel[step_t, step_h, step_w]
    return summed

def reference(teacher_in, teacher_weights, student_in, depth_weights, point_weights, project_weight):
    target = teacher_in
    for block_index in range(teacher_weights.shape[0]):
        current = target.astype(jnp.float32)
        active = jax.nn.silu(root_norm(current)).astype(jnp.bfloat16)
        middle = dense_conv(causal_pad(active), teacher_weights[block_index, 0])
        second = jax.nn.silu(root_norm(middle)).astype(jnp.bfloat16)
        target = (current + dense_conv(causal_pad(second), teacher_weights[block_index, 1])).astype(jnp.bfloat16)
    channels = student_in.shape[-1]
    current = student_in.astype(jnp.float32)
    stored = []
    for layer_index in range(depth_weights.shape[0]):
        active = jax.nn.silu(current).astype(jnp.bfloat16)
        spread = depthwise(causal_pad(active), depth_weights[layer_index]).astype(jnp.bfloat16)
        stored.append(current)
        mixed = jnp.dot(spread.reshape(-1, channels), point_weights[layer_index], preferred_element_type=jnp.float32)
        current = current + mixed.reshape(current.shape)
    projected = jnp.dot(current.astype(jnp.bfloat16).reshape(-1, channels), project_weight, preferred_element_type=jnp.float32)
    mismatch = (projected - target.astype(jnp.float32).reshape(projected.shape)).astype(jnp.bfloat16)
    gradient = lax.dot_general(mismatch, project_weight, (((1,), (1,)), ((), ())), preferred_element_type=jnp.float32).reshape(current.shape)
    for layer_index in reversed(range(depth_weights.shape[0])):
        backward = lax.dot_general(gradient.astype(jnp.bfloat16).reshape(-1, channels), point_weights[layer_index], (((1,), (1,)), ((), ())), preferred_element_type=jnp.float32)
        backward = backward.astype(jnp.bfloat16).reshape(current.shape)
        flipped = depth_weights[layer_index][::-1, ::-1, ::-1]
        spread_back = depthwise(future_pad(backward), flipped)
        gradient = gradient + spread_back * silu_slope(stored[layer_index])
    return gradient.astype(jnp.bfloat16)
```

```python
import jax
import jax.numpy as jnp
from jax import lax
from jax.experimental import pallas as pl
from jax.experimental.pallas import tpu as pltpu
from jax.sharding import PartitionSpec as P

MESH = pl.DeviceIdType.MESH
F32, BF16 = jnp.float32, jnp.bfloat16
SIDES = [(0, -1), (0, 1), (-1, 0), (1, 0), (-1, -1), (-1, 1), (1, -1), (1, 1)]
CT, CS, WIDE = 192, 128, 256
NTA, NHA, NWA = 4, 4, 32
GRID_R, GRID_C = NTA * NHA, NWA
TRANSPOSED = (((1,), (1,)), ((), ()))


def rational(x):
    gate = 0.5 * jnp.tanh(0.5 * x) + 0.5
    return x * gate


def act(s):
    gate = 0.5 * jnp.tanh(0.5 * s) + 0.5
    u = s * gate
    return u, gate + u * (1.0 - gate)


def silu_norm(x):
    scale = lax.rsqrt(jnp.sum(x * x, axis=-1, keepdims=True) * (1.0 / CT) + 1e-06)
    return rational(x * scale)


def shifted(v, by, frames):
    if by > 0:
        return jnp.where(frames >= by, pltpu.roll(v, by, v.ndim - 2), 0.0)
    return jnp.where(frames < 8 + by, pltpu.roll(v, 8 + by, v.ndim - 2), 0.0)


def kernel(
    tin, tw, sin, dw, pw, proj, out,
    xin, xf, xt, hact, hsec, af, lhs, wb, pp,
    rin, rf, s0f, s2f, u12, u10, mm10, mm8, sl0, sl1, sl2, sl3, d10, d8,
    h0, h2, h4, h6, gf, s4b, mb, pr, ob, dwv, pwv, projv,
    wsem, xsend, xrecv, rsend, rrecv, osend, orecv, hsend, hrecv,
):
    ta, ha, wa = lax.axis_index("ta"), lax.axis_index("ha"), lax.axis_index("wa")
    row, col = ha * NTA + ta, wa
    band, line = lax.div(wa, 8), lax.rem(wa, 8)
    has_self = band == ta

    def at(a, b, c):
        return {"ta": a, "ha": b, "wa": c}

    def near(dr, dc):
        r = row + dr
        return at(lax.rem(r + GRID_R, NTA), lax.div(r + GRID_R, NTA) - NHA, col + dc)

    def there(dr, dc):
        r, c = row + dr, col + dc
        return (r >= 0) & (r < GRID_R) & (c >= 0) & (c < GRID_C)

    weights = []
    for b in range(2):
        for i in range(3):
            weights.append(
                pltpu.make_async_copy(
                    tw.at[0, b, i], wb.at[b, i, :, :, 0:CT, :], wsem.at[b * 3 + i]
                )
            )
    small = [
        pltpu.make_async_copy(dw, dwv, wsem.at[6]),
        pltpu.make_async_copy(pw, pwv, wsem.at[7]),
        pltpu.make_async_copy(proj, projv, wsem.at[8]),
    ]
    for copy in small + weights:
        copy.start()

    for buf in (hact, hsec, h0, h2, h4, h6, af):
        buf[...] = jnp.zeros_like(buf)
    wb[:, :, :, :, CT:WIDE, :] = jnp.zeros((2, 3, 3, 3, WIDE - CT, CT), BF16)

    barrier = pltpu.get_barrier_semaphore()

    def greet(device):
        pl.semaphore_signal(barrier, inc=1, device_id=device, device_id_type=MESH)

    @pl.loop(0, NWA)
    def _(c):
        @pl.when(jnp.logical_not(has_self & (c == wa)))
        def _():
            greet(at(band, ha, c))

    @pl.loop(0, 32)
    def _(m):
        x, y = lax.div(m, 8), ta * 8 + lax.rem(m, 8)

        @pl.when(jnp.logical_not((x == ta) & (y == wa)))
        def _():
            greet(at(x, ha, y))

    for dx in range(1, NTA):
        greet(at(lax.rem(ta + dx, NTA), ha, wa))
    near_count = 0
    for dr, dc in SIDES:
        present = there(dr, dc)
        near_count = near_count + present.astype(jnp.int32)

        @pl.when(present)
        def _():
            greet(near(dr, dc))

    pl.semaphore_wait(barrier, 64 - 2 * has_self.astype(jnp.int32) + 3 + near_count)

    def slab_copy(dx):
        x = lax.rem(ta + dx, NTA)
        return pltpu.make_async_remote_copy(
            src_ref=tin.at[:, pl.ds(x * 8, 8)],
            dst_ref=xin.at[pl.ds(ta * 2, 2)],
            send_sem=xsend.at[dx],
            recv_sem=xrecv.at[dx],
            device_id=at(x, ha, wa),
            device_id_type=MESH,
        )

    own_slab = pltpu.make_async_copy(
        tin.at[:, pl.ds(ta * 8, 8)], xin.at[pl.ds(ta * 2, 2)], xrecv.at[0]
    )
    for dx in range(1, NTA):
        slab_copy(dx).start()
    own_slab.start()

    @pl.loop(0, NWA)
    def _(step):
        c = lax.rem(wa + step, NWA)
        itself = has_self & (step == 0)

        @pl.when(itself)
        def _():
            pltpu.make_async_copy(sin.at[:, c], rin.at[pl.ds(ta * 2, 2), line], rrecv).start()

        @pl.when(jnp.logical_not(itself))
        def _():
            pltpu.make_async_remote_copy(
                src_ref=sin.at[:, c],
                dst_ref=rin.at[pl.ds(ta * 2, 2), line],
                send_sem=rsend,
                recv_sem=rrecv,
                device_id=at(band, ha, c),
                device_id_type=MESH,
            ).start()

    def side_copy(buf, k, slot, d):
        dr, dc = SIDES[d]
        source = {-1: (k, k), 0: (k, 8), 1: (8, k)}
        target = {-1: (8 + k, k), 0: (k, 8), 1: (0, k)}
        rs, cs, rt, ct = source[dr], source[dc], target[dr], target[dc]
        return pltpu.make_async_remote_copy(
            src_ref=buf.at[pl.ds(*rs), pl.ds(*cs)],
            dst_ref=buf.at[pl.ds(*rt), pl.ds(*ct)],
            send_sem=hsend.at[slot, d],
            recv_sem=hrecv.at[slot, d],
            device_id=near(dr, dc),
            device_id_type=MESH,
        )

    def send(buf, k, slot):
        for d, (dr, dc) in enumerate(SIDES):
            @pl.when(there(dr, dc))
            def _():
                side_copy(buf, k, slot, d).start()

    def receive(buf, k, slot):
        for d, (dr, dc) in enumerate(SIDES):
            @pl.when(there(-dr, -dc))
            def _():
                side_copy(buf, k, slot, d).wait_recv()

    def drain(buf, k, slot):
        for d, (dr, dc) in enumerate(SIDES):
            @pl.when(there(dr, dc))
            def _():
                side_copy(buf, k, slot, d).wait_send()

    def ring(k):
        full = 8 + 2 * k
        return [
            (slice(0, k), slice(0, full)),
            (slice(8 + k, full), slice(0, full)),
            (slice(k, 8 + k), slice(0, k)),
            (slice(k, 8 + k), slice(8 + k, full)),
        ]

    def clear_outside(buf):
        @pl.when(row == 0)
        def _():
            buf[0] = jnp.zeros_like(buf[0])

        @pl.when(row == GRID_R - 1)
        def _():
            buf[9] = jnp.zeros_like(buf[9])

        @pl.when(col == 0)
        def _():
            buf[:, 0] = jnp.zeros_like(buf[:, 0])

        @pl.when(col == GRID_C - 1)
        def _():
            buf[:, 9] = jnp.zeros_like(buf[:, 9])

    frames = lax.broadcasted_iota(jnp.int32, (1, 8, CS), 1)
    wide_frames = lax.broadcasted_iota(jnp.int32, (1, 8, CT), 1)

    def taps(src, h, width, n, flip):
        acc = [None] * 3
        for j in range(3):
            for l in range(3):
                x = src[h + j, l : l + width]
                for i in range(3):
                    jj, ll = (2 - j, 2 - l) if flip else (j, l)
                    term = x * dwv[n, i, jj, ll : ll + 1, :].reshape(1, 1, CS)
                    acc[i] = term if acc[i] is None else acc[i] + term
        sign = -1 if flip else 1
        return acc[2] + shifted(acc[1], sign, frames) + shifted(acc[0], 2 * sign, frames)

    def conv(b):
        for j in range(3):
            for l in range(3):
                at_lane = (j * 3 + l) * WIDE
                lhs[:, at_lane : at_lane + WIDE] = (
                    af[j : j + 8, l : l + 8].reshape(512, WIDE).astype(BF16)
                )
        for i in range(3):
            weights[b * 3 + i].wait()
            pp[i] = jnp.dot(
                lhs[...], wb[b, i].reshape(9 * WIDE, CT), preferred_element_type=F32
            )

    def conv_row(h):
        p = [pp[i, pl.ds(h * 64, 64)].reshape(8, 8, CT) for i in range(3)]
        return p[2] + shifted(p[1], 1, wide_frames) + shifted(p[0], 2, wide_frames)

    own_slab.wait()
    for dx in range(1, NTA):
        slab_copy(dx).wait_recv()
    xall = xin[...].astype(F32).reshape(512, CT)
    xf[0] = xall[:, 0:CS]
    xf[1, :, 0 : CT - CS] = xall[:, CS:CT]

    @pl.loop(0, 8)
    def _(h):
        for w in range(8):
            place = pl.ds(h * 8 + w, 8, stride=64)
            x = jnp.concatenate([xf[0, place, :], xf[1, place, :][:, 0 : CT - CS]], axis=-1)
            xt[h, w] = x
            a = silu_norm(x)
            hact[h + 1, w + 1] = a.astype(BF16)
            af[h + 1, w + 1, :, 0:CT] = a

    send(hact, 1, 0)

    pltpu.make_async_copy(rin, rin, rrecv).wait()
    rf[...] = rin[...].astype(F32).reshape(512, CS)

    @pl.loop(0, 8)
    def _(h):
        for w in range(8):
            s = rf[pl.ds(h * 8 + w, 8, stride=64), :]
            s0f[h + 2, w + 2] = s
            h0[h + 2, w + 2] = s.astype(BF16)
            u, slope = act(s)
            u12[h + 2, w + 2] = u
            sl0[h, w] = slope

    send(h0, 2, 1)

    receive(hact, 1, 0)
    for rows, cols in ring(1):
        af[rows, cols, :, 0:CT] = hact[rows, cols].astype(F32)
    conv(0)

    @pl.loop(0, 8)
    def _(h):
        a = silu_norm(conv_row(h))
        hsec[h + 1, 1:9] = a.astype(BF16)
        af[h + 1, 1:9, :, 0:CT] = a

    send(hsec, 1, 2)

    for copy in small:
        copy.wait()

    def border(buf, field):
        for rows, cols in ring(2):
            s = buf[rows, cols].astype(F32)
            field[rows, cols] = s
            u12[rows, cols] = act(s)[0]

    def wide_layer(n, field, slope_buf):
        @pl.loop(0, 10)
        def _(h):
            d10[h] = taps(u12, h, 10, n, False).reshape(80, CS).astype(BF16)

        mm10[...] = jnp.dot(
            d10[...].reshape(800, CS), pwv[n], preferred_element_type=F32
        ).reshape(10, 10, 8, CS)

        @pl.loop(0, 10)
        def _(h):
            s = field[h + 1, 1:11] + mm10[h]
            mm10[h] = s
            u, slope = act(s)
            u10[h] = u
            slope_buf[h] = slope

        clear_outside(u10)

    def narrow_layer(n):
        @pl.loop(0, 8)
        def _(h):
            d8[h] = taps(u10, h, 8, n, False).reshape(64, CS).astype(BF16)

        mm8[...] = jnp.dot(
            d8[...].reshape(512, CS), pwv[n], preferred_element_type=F32
        ).reshape(8, 8, 8, CS)

    receive(h0, 2, 1)
    border(h0, s0f)
    wide_layer(0, s0f, sl1)
    narrow_layer(1)

    @pl.loop(0, 8)
    def _(h):
        s = mm10[h + 1, 1:9] + mm8[h]
        s2f[h + 2, 2:10] = s
        h2[h + 2, 2:10] = s.astype(BF16)
        u, slope = act(s)
        u12[h + 2, 2:10] = u
        sl2[h] = slope

    send(h2, 2, 3)

    receive(hsec, 1, 2)
    for rows, cols in ring(1):
        af[rows, cols, :, 0:CT] = hsec[rows, cols].astype(F32)
    conv(1)

    receive(h2, 2, 3)
    border(h2, s2f)
    wide_layer(2, s2f, sl3)
    narrow_layer(3)

    @pl.loop(0, 8)
    def _(h):
        s4b[h] = (mm10[h + 1, 1:9] + mm8[h]).reshape(64, CS).astype(BF16)

    pr[...] = jnp.dot(
        s4b[...].reshape(512, CS), projv[...], preferred_element_type=F32
    ).reshape(8, 64, CT)

    @pl.loop(0, 8)
    def _(h):
        target = (xt[h] + conv_row(h)).reshape(64, CT)
        mb[h] = (pr[h] - target).astype(BF16)

    mm8[...] = lax.dot_general(
        mb[...].reshape(512, CT), projv[...], TRANSPOSED, preferred_element_type=F32
    ).reshape(8, 8, 8, CS)

    @pl.loop(0, 8)
    def _(h):
        g = mm8[h]
        gf[h + 2, 2:10] = g
        h4[h + 2, 2:10] = g.astype(BF16)

    send(h4, 2, 4)

    def wide_back(n, buf, slot, slope_buf):
        receive(buf, 2, slot)
        for rows, cols in ring(2):
            gf[rows, cols] = buf[rows, cols].astype(F32)
        u12[...] = lax.dot_general(
            gf[...].reshape(1152, CS).astype(BF16), pwv[n], TRANSPOSED, preferred_element_type=F32
        ).reshape(12, 12, 8, CS)

        @pl.loop(0, 10)
        def _(h):
            mm10[h] = gf[h + 1, 1:11] + taps(u12, h, 10, n, True) * slope_buf[h]

        clear_outside(mm10)
        u10[...] = lax.dot_general(
            mm10[...].reshape(800, CS).astype(BF16),
            pwv[n - 1],
            TRANSPOSED,
            preferred_element_type=F32,
        ).reshape(10, 10, 8, CS)

    wide_back(3, h4, 4, sl3)

    @pl.loop(0, 8)
    def _(h):
        g = mm10[h + 1, 1:9] + taps(u10, h, 8, 2, True) * sl2[h]
        gf[h + 2, 2:10] = g
        h6[h + 2, 2:10] = g.astype(BF16)

    send(h6, 2, 5)
    wide_back(1, h6, 5, sl1)

    @pl.loop(0, 8)
    def _(h):
        g = mm10[h + 1, 1:9] + taps(u10, h, 8, 0, True) * sl0[h]
        rf[pl.ds(h * 64, 64)] = g.reshape(64, CS)

    @pl.loop(0, 8)
    def _(h):
        for t in range(8):
            ob[t, h] = rf[pl.ds(h * 64 + t, 8, stride=8), :].astype(BF16)

    @pl.loop(0, 32)
    def _(m):
        spot = lax.rem(m + wa, 32)
        x, h = lax.div(spot, 8), lax.rem(spot, 8)
        itself = (x == ta) & (ta * 8 + h == wa)

        @pl.when(itself)
        def _():
            pltpu.make_async_copy(ob.at[pl.ds(x * 2, 2), h], out.at[:, wa], orecv).start()

        @pl.when(jnp.logical_not(itself))
        def _():
            pltpu.make_async_remote_copy(
                src_ref=ob.at[pl.ds(x * 2, 2), h],
                dst_ref=out.at[:, wa],
                send_sem=osend,
                recv_sem=orecv,
                device_id=at(x, ha, ta * 8 + h),
                device_id_type=MESH,
            ).start()

    for buf, k, slot in (
        (hact, 1, 0), (h0, 2, 1), (hsec, 1, 2), (h2, 2, 3), (h4, 2, 4), (h6, 2, 5)
    ):
        drain(buf, k, slot)
    for dx in range(1, NTA):
        slab_copy(dx).wait_send()
    pltpu.make_async_copy(out, out, orecv).wait()

    for sem in (rsend, osend):
        @pl.when(has_self)
        def _():
            part = sin.at[:, 0:31]
            pltpu.make_async_copy(part, part, sem).wait()

        @pl.when(jnp.logical_not(has_self))
        def _():
            pltpu.make_async_copy(sin, sin, sem).wait()


def on_device(tin, tw, sin, dw, pw, proj):
    anywhere = pl.BlockSpec(memory_space=pl.ANY)
    tile = lambda rows, cols, c, kind: pltpu.VMEM((rows, cols, 8, c), kind)
    dma = pltpu.SemaphoreType.DMA
    scratch = [
        pltpu.VMEM((8, 8, 8, CT), BF16),
        pltpu.VMEM((2, 512, CS), F32),
        tile(8, 8, CT, F32),
        tile(10, 10, CT, BF16),
        tile(10, 10, CT, BF16),
        tile(10, 10, WIDE, F32),
        pltpu.VMEM((512, 9 * WIDE), BF16),
        pltpu.VMEM((2, 3, 3, 3, WIDE, CT), BF16),
        pltpu.VMEM((3, 512, CT), F32),
        pltpu.VMEM((8, 8, 8, CS), BF16),
        pltpu.VMEM((512, CS), F32),
        tile(12, 12, CS, F32),
        tile(12, 12, CS, F32),
        tile(12, 12, CS, F32),
        tile(10, 10, CS, F32),
        tile(10, 10, CS, F32),
        tile(8, 8, CS, F32),
        tile(8, 8, CS, F32),
        tile(10, 10, CS, F32),
        tile(8, 8, CS, F32),
        tile(10, 10, CS, F32),
        pltpu.VMEM((10, 80, CS), BF16),
        pltpu.VMEM((8, 64, CS), BF16),
        tile(12, 12, CS, BF16),
        tile(12, 12, CS, BF16),
        tile(12, 12, CS, BF16),
        tile(12, 12, CS, BF16),
        tile(12, 12, CS, F32),
        pltpu.VMEM((8, 64, CS), BF16),
        pltpu.VMEM((8, 64, CT), BF16),
        pltpu.VMEM((8, 64, CT), F32),
        pltpu.VMEM((8, 8, 8, CS), BF16),
        pltpu.VMEM((4, 3, 3, 3, CS), F32),
        pltpu.VMEM((4, CS, CS), BF16),
        pltpu.VMEM((CS, CT), BF16),
        dma((9,)),
        dma((NTA,)),
        dma((NTA,)),
        dma(()),
        dma(()),
        dma(()),
        dma(()),
        dma((6, 8)),
        dma((6, 8)),
    ]
    result = pl.pallas_call(
        kernel,
        out_shape=jax.ShapeDtypeStruct((2, 32, 8, CS), BF16),
        in_specs=[anywhere] * 6,
        out_specs=anywhere,
        scratch_shapes=scratch,
        compiler_params=pltpu.CompilerParams(
            collective_id=0, has_side_effects=True, vmem_limit_bytes=56 * 1024 * 1024
        ),
    )(tin, tw, sin.reshape(2, 32, 8, CS), dw, pw, proj)
    return result.reshape(2, 1, 256, CS)


def solution(mesh):
    rows = P("ta", ("ha", "wa"), None, None)
    return jax.shard_map(
        on_device,
        mesh=mesh,
        in_specs=(P("ta", "ha", "wa", None), P(), rows, P(), P(), P()),
        out_specs=rows,
        check_vma=False,
    )
```

```python
import jax
import jax.numpy as jnp
from jax import lax
from jax.experimental import pallas as pl
from jax.experimental.pallas import tpu as pltpu
from jax.sharding import PartitionSpec as P

MESH = pl.DeviceIdType.MESH
F32, BF16 = jnp.float32, jnp.bfloat16
SIDES = [(0, -1), (0, 1), (-1, 0), (1, 0), (-1, -1), (-1, 1), (1, -1), (1, 1)]
CT, CS, WIDE = 192, 128, 256
TH, TW = 4, 16
GRID_R, GRID_C = 32, 16
TRANSPOSED = (((1,), (1,)), ((), ()))


def rational(x):
    gate = 0.5 * jnp.tanh(0.5 * x) + 0.5
    return x * gate


def act(s):
    gate = 0.5 * jnp.tanh(0.5 * s) + 0.5
    u = s * gate
    return u, gate + u * (1.0 - gate)


def silu_norm(x):
    scale = lax.rsqrt(jnp.sum(x * x, axis=-1, keepdims=True) * (1.0 / CT) + 1e-06)
    return rational(x * scale)


def shifted(v, by, frames):
    if by > 0:
        return jnp.where(frames >= by, pltpu.roll(v, by, v.ndim - 2), 0.0)
    return jnp.where(frames < 8 + by, pltpu.roll(v, 8 + by, v.ndim - 2), 0.0)


def kernel(
    tin, tw, sin, dw, pw, proj, out,
    xin, xf, xt, hact, hsec, af, lhs, wb, pp,
    rin, rf, s0f, s2f, u20, u18, d18, mm18, d16, mm16, sl0, sl1, sl2,
    h0, h2, hs, hg, gf, eb, g22, g20, s4b, mb, pr, ob, dwv, pwv, projv,
    wsem, xsend, xrecv, rsend, rrecv, osend, orecv, hsend, hrecv,
):
    ta, ha, wa = lax.axis_index("ta"), lax.axis_index("ha"), lax.axis_index("wa")
    z, low = lax.div(wa, 4), lax.rem(wa, 4)

    def bent(p):
        return jnp.where(p < 2, p, 5 - p)

    def place(a, b):
        p = bent(b)
        return a * 4 + jnp.where(lax.rem(a, 2) == 0, p, 3 - p)

    row, col = ha * 8 + z, place(ta, low)

    def at(a, b, c):
        return {"ta": a, "ha": b, "wa": c}

    def owner(r, c):
        a, p = lax.div(c, 4), lax.rem(c, 4)
        p = bent(jnp.where(lax.rem(a, 2) == 0, p, 3 - p))
        return at(a, lax.div(r, 8), lax.rem(r, 8) * 4 + p)

    def near(dr, dc):
        return owner(row + dr, col + dc)

    def there(dr, dc):
        r, c = row + dr, col + dc
        return (r >= 0) & (r < GRID_R) & (c >= 0) & (c < GRID_C)

    weights = []
    for b in range(2):
        for i in range(3):
            weights.append(
                pltpu.make_async_copy(
                    tw.at[0, b, i], wb.at[b, i, :, :, 0:CT, :], wsem.at[b * 3 + i]
                )
            )
    small = [
        pltpu.make_async_copy(dw, dwv, wsem.at[6]),
        pltpu.make_async_copy(pw, pwv, wsem.at[7]),
        pltpu.make_async_copy(proj, projv, wsem.at[8]),
    ]
    for copy in small + weights:
        copy.start()

    def clear_outside(buf, k):
        @pl.when(row == 0)
        def _():
            buf[0:k] = jnp.zeros_like(buf[0:k])

        @pl.when(row == GRID_R - 1)
        def _():
            buf[TH + k :] = jnp.zeros_like(buf[TH + k :])

        @pl.when(col == 0)
        def _():
            buf[:, 0:k] = jnp.zeros_like(buf[:, 0:k])

        @pl.when(col == GRID_C - 1)
        def _():
            buf[:, TW + k :] = jnp.zeros_like(buf[:, TW + k :])

    halos = ((hact, 1, 0), (h0, 2, 1), (hsec, 1, 2), (h2, 2, 3), (hs, 3, 4), (hg, 4, 5))
    for buf, k, _ in halos:
        clear_outside(buf, k)

    barrier = pltpu.get_barrier_semaphore()

    def greet(device):
        pl.semaphore_signal(barrier, inc=1, device_id=device, device_id_type=MESH)

    spread_count = jnp.where(lax.div(wa, 2) == col, 7, 8)
    for step in range(8):
        r = ha * 8 + lax.rem(z + step, 8)

        @pl.when(jnp.logical_not((r == row) & (lax.div(wa, 2) == col)))
        def _():
            greet(owner(r, lax.div(wa, 2)))

    for step in range(8):
        a, b = step // 2, 2 * col + step % 2

        @pl.when(jnp.logical_not((a == ta) & (b == wa)))
        def _():
            greet(at(a, ha, b))

    gather_count = jnp.where(lax.div(wa, 2) == col, 7, 8)
    for step in range(1, 16):
        greet(owner(row, lax.rem(col + step, 16)))
    near_count = 0
    for dr, dc in SIDES:
        present = there(dr, dc)
        near_count = near_count + present.astype(jnp.int32)

        @pl.when(present)
        def _():
            greet(near(dr, dc))

    af[:, :, :, CS:WIDE] = jnp.zeros((TH + 2, TW + 2, 8, WIDE - CS), F32)
    wb[:, :, :, :, CT:WIDE, :] = jnp.zeros((2, 3, 3, 3, WIDE - CT, CT), BF16)
    pl.semaphore_wait(barrier, 15 + spread_count + gather_count + near_count)

    own_patch = pltpu.make_async_copy(
        tin.at[:, pl.ds(z * TH, TH)], xin.at[pl.ds(ta * 2, 2), :, lax.rem(wa, 2)], xrecv
    )
    patch_self = lax.div(wa, 2) == col
    for step in range(8):
        to = lax.rem(z + step, 8)

        def send_patch():
            pltpu.make_async_remote_copy(
                src_ref=tin.at[:, pl.ds(to * TH, TH)],
                dst_ref=xin.at[pl.ds(ta * 2, 2), :, lax.rem(wa, 2)],
                send_sem=xsend,
                recv_sem=xrecv,
                device_id=owner(ha * 8 + to, lax.div(wa, 2)),
                device_id_type=MESH,
            ).start()

        if step:
            send_patch()
        else:
            pl.when(patch_self)(own_patch.start)
            pl.when(jnp.logical_not(patch_self))(send_patch)

    pltpu.make_async_copy(
        sin.at[:, pl.ds(col * 2, 2)], rin.at[pl.ds(ta * 2, 2), low], rrecv
    ).start()
    for step in range(1, 16):
        c = lax.rem(col + step, 16)
        pltpu.make_async_remote_copy(
            src_ref=sin.at[:, pl.ds(c * 2, 2)],
            dst_ref=rin.at[pl.ds(ta * 2, 2), low],
            send_sem=rsend,
            recv_sem=rrecv,
            device_id=owner(row, c),
            device_id_type=MESH,
        ).start()

    def side_copy(buf, k, slot, d):
        dr, dc = SIDES[d]

        def source(side, size):
            return pl.ds(*{-1: (k, k), 0: (k, size), 1: (size, k)}[side])

        def target(side, size):
            return pl.ds(*{-1: (size + k, k), 0: (k, size), 1: (0, k)}[side])

        return pltpu.make_async_remote_copy(
            src_ref=buf.at[source(dr, TH), source(dc, TW)],
            dst_ref=buf.at[target(dr, TH), target(dc, TW)],
            send_sem=hsend.at[slot, d],
            recv_sem=hrecv.at[slot, d],
            device_id=near(dr, dc),
            device_id_type=MESH,
        )

    def send(buf, k, slot):
        for d, (dr, dc) in enumerate(SIDES):
            @pl.when(there(dr, dc))
            def _():
                side_copy(buf, k, slot, d).start()

    def receive(buf, k, slot):
        for d, (dr, dc) in enumerate(SIDES):
            @pl.when(there(-dr, -dc))
            def _():
                side_copy(buf, k, slot, d).wait_recv()

    def drain(buf, k, slot):
        for d, (dr, dc) in enumerate(SIDES):
            @pl.when(there(dr, dc))
            def _():
                side_copy(buf, k, slot, d).wait_send()

    def ring(k):
        rows, cols = TH + 2 * k, TW + 2 * k
        return [
            (slice(0, k), slice(0, cols)),
            (slice(TH + k, rows), slice(0, cols)),
            (slice(k, TH + k), slice(0, k)),
            (slice(k, TH + k), slice(TW + k, cols)),
        ]

    frames = lax.broadcasted_iota(jnp.int32, (1, 8, CS), 1)
    wide_frames = lax.broadcasted_iota(jnp.int32, (1, 8, CT), 1)

    def taps(src, h, start, width, n, flip):
        acc = [None] * 3
        for j in range(3):
            for l in range(3):
                x = src[h + j, start + l : start + l + width]
                for i in range(3):
                    jj, ll = (2 - j, 2 - l) if flip else (j, l)
                    term = x * dwv[i, jj, ll, n : n + 1, :].reshape(1, 1, CS)
                    acc[i] = term if acc[i] is None else acc[i] + term
        sign = -1 if flip else 1
        return acc[2] + shifted(acc[1], sign, frames) + shifted(acc[0], 2 * sign, frames)

    def conv(b):
        for j in range(3):
            for l in range(3):
                at_lane = (j * 3 + l) * WIDE
                lhs[:, at_lane : at_lane + WIDE] = (
                    af[j : j + TH, l : l + TW].reshape(512, WIDE).astype(BF16)
                )
        for i in range(3):
            weights[b * 3 + i].wait()
            pp[i] = jnp.dot(
                lhs[...], wb[b, i].reshape(9 * WIDE, CT), preferred_element_type=F32
            )

    def conv_row(m):
        p = [pp[i, pl.ds(m * 64, 64)].reshape(8, 8, CT) for i in range(3)]
        return p[2] + shifted(p[1], 1, wide_frames) + shifted(p[0], 2, wide_frames)

    pltpu.make_async_copy(rin, rin, rrecv).wait()
    rf[...] = rin[...].astype(F32).reshape(512, CS)

    @pl.loop(0, TH)
    def _(h):
        for w in range(TW):
            s = rf[pl.ds(h * TW + w, 8, stride=64), :]
            s0f[h + 2, w + 2] = s
            h0[h + 2, w + 2] = s.astype(BF16)
            u, slope = act(s)
            u20[h + 2, w + 2] = u
            sl0[h, w] = slope

    send(h0, 2, 1)

    pltpu.make_async_copy(xin, xin, xrecv).wait()
    xall = xin[...].astype(F32).reshape(512, CT)
    xf[0] = xall[:, 0:CS]
    xf[1, :, 0 : CT - CS] = xall[:, CS:CT]

    @pl.loop(0, TH)
    def _(h):
        for w in range(TW):
            spot = pl.ds(h * TW + w, 8, stride=64)
            x = jnp.concatenate([xf[0, spot, :], xf[1, spot, :][:, 0 : CT - CS]], axis=-1)
            xt[h, w] = x
            a = silu_norm(x)
            hact[h + 1, w + 1] = a.astype(BF16)
            af[h + 1, w + 1, :, 0:CT] = a

    send(hact, 1, 0)

    for copy in small:
        copy.wait()

    def wide_layer(n, field):
        @pl.loop(0, TH + 2)
        def _(h):
            for w in (0, 9):
                d18[h, w : w + 9] = taps(u20, h, w, 9, n, False)

        mm18[...] = jnp.dot(
            d18[...].reshape(864, CS).astype(BF16), pwv[n], preferred_element_type=F32
        ).reshape(6, 18, 8, CS)

        @pl.loop(0, TH + 2)
        def _(h):
            s = field[h + 1, 1:19] + mm18[h]
            mm18[h] = s
            u, slope = act(s)
            u18[h] = u
            sl1[h] = slope

        clear_outside(u18, 1)

    def narrow_layer(n):
        @pl.loop(0, TH)
        def _(h):
            for w in (0, 8):
                d16[h, w : w + 8] = taps(u18, h, w, 8, n, False)

        mm16[...] = jnp.dot(
            d16[...].reshape(512, CS).astype(BF16), pwv[n], preferred_element_type=F32
        ).reshape(4, 16, 8, CS)

    receive(h0, 2, 1)
    for rows, cols in ring(2):
        s = h0[rows, cols].astype(F32)
        s0f[rows, cols] = s
        u20[rows, cols] = act(s)[0]
    wide_layer(0, s0f)
    narrow_layer(1)

    @pl.loop(0, TH)
    def _(h):
        s = mm18[h + 1, 1:17] + mm16[h]
        s2f[h + 2, 2:18] = s
        h2[h + 2, 2:18] = s.astype(BF16)
        u, slope = act(s)
        u20[h + 2, 2:18] = u
        sl2[h + 2, 2:18] = slope

    send(h2, 2, 3)

    receive(hact, 1, 0)
    for rows, cols in ring(1):
        af[rows, cols, :, 0:CT] = hact[rows, cols].astype(F32)
    conv(0)

    @pl.loop(0, 8)
    def _(m):
        h, w = lax.div(m, 2), lax.rem(m, 2) * 8
        a = silu_norm(conv_row(m))
        hsec[h + 1, pl.ds(w + 1, 8)] = a.astype(BF16)
        af[h + 1, pl.ds(w + 1, 8), :, 0:CT] = a

    send(hsec, 1, 2)

    receive(h2, 2, 3)
    for rows, cols in ring(2):
        s = h2[rows, cols].astype(F32)
        s2f[rows, cols] = s
        u, slope = act(s)
        u20[rows, cols] = u
        sl2[rows, cols] = slope

    @pl.loop(0, TH + 2)
    def _(h):
        for w in (0, 9):
            d18[h, w : w + 9] = taps(u20, h, w, 9, 2, False)

    mm18[...] = jnp.dot(
        d18[...].reshape(864, CS).astype(BF16), pwv[2], preferred_element_type=F32
    ).reshape(6, 18, 8, CS)

    @pl.loop(0, TH + 2)
    def _(h):
        s = s2f[h + 1, 1:19] + mm18[h]
        mm18[h] = s
        u, slope = act(s)
        u18[h] = u
        d18[h] = slope

    hs[3:7, 3:19] = d18[1:5, 1:17].astype(BF16)
    send(hs, 3, 4)
    clear_outside(u18, 1)
    narrow_layer(3)
    s4b[...] = (mm18[1:5, 1:17] + mm16[...]).reshape(512, CS).astype(BF16)

    pr[...] = lax.dot_general(s4b[...], projv[...], TRANSPOSED, preferred_element_type=F32)

    receive(hsec, 1, 2)
    for rows, cols in ring(1):
        af[rows, cols, :, 0:CT] = hsec[rows, cols].astype(F32)
    conv(1)

    @pl.loop(0, 8)
    def _(m):
        h, w = lax.div(m, 2), lax.rem(m, 2) * 8
        target = (xt[h, pl.ds(w, 8)] + conv_row(m)).reshape(64, CT)
        span = pl.ds(m * 64, 64)
        mb[span] = (pr[span] - target).astype(BF16)

    g = jnp.dot(mb[...], projv[...], preferred_element_type=F32).reshape(4, 16, 8, CS)
    gf[4:8, 4:20] = g
    hg[4:8, 4:20] = g.astype(BF16)
    send(hg, 4, 5)

    receive(hs, 3, 4)
    receive(hg, 4, 5)
    for rows, cols in ring(4):
        gf[rows, cols] = hg[rows, cols].astype(F32)

    def back(n, source, k):
        rows, cols = TH + 2 * k, TW + 2 * k
        eb[0:rows, 0:cols] = lax.dot_general(
            source[...].reshape(rows * cols * 8, CS).astype(BF16),
            pwv[n],
            TRANSPOSED,
            preferred_element_type=F32,
        ).reshape(rows, cols, 8, CS)

    back(3, gf, 4)

    @pl.loop(0, 10)
    def _(h):
        for w in (0, 11):
            slope = hs[h, w : w + 11].astype(F32)
            g22[h, w : w + 11] = (
                gf[h + 1, w + 1 : w + 12] + taps(eb, h, w, 11, 3, True) * slope
            )

    clear_outside(g22, 3)
    back(2, g22, 3)

    @pl.loop(0, 8)
    def _(h):
        for w in (0, 10):
            g20[h, w : w + 10] = (
                g22[h + 1, w + 1 : w + 11]
                + taps(eb, h, w, 10, 2, True) * sl2[h, w : w + 10]
            )

    clear_outside(g20, 2)
    back(1, g20, 2)

    @pl.loop(0, 6)
    def _(h):
        for w in (0, 9):
            d18[h, w : w + 9] = (
                g20[h + 1, w + 1 : w + 10]
                + taps(eb, h, w, 9, 1, True) * sl1[h, w : w + 9]
            )

    clear_outside(d18, 1)
    back(0, d18, 1)

    @pl.loop(0, 4)
    def _(h):
        for w in (0, 8):
            g = (
                d18[h + 1, w + 1 : w + 9]
                + taps(eb, h, w, 8, 0, True) * sl0[h, w : w + 8]
            )
            rf[pl.ds(h * 128 + w * 8, 64)] = g.reshape(64, CS)

    @pl.loop(0, TH)
    def _(h):
        for half in range(2):
            for t in range(8):
                ob[t, h, half] = rf[
                    pl.ds(h * 128 + half * 64 + t, 8, stride=8), :
                ].astype(BF16)

    for step in range(16):
        x, y = lax.rem(ta + step // 4, 4), lax.rem(low + step % 4, 4)
        source = ob.at[pl.ds(x * 2, 2), y]
        if step:
            pltpu.make_async_remote_copy(
                src_ref=source,
                dst_ref=out.at[:, pl.ds(col * 2, 2)],
                send_sem=osend,
                recv_sem=orecv,
                device_id=at(x, ha, z * 4 + y),
                device_id_type=MESH,
            ).start()
        else:
            pltpu.make_async_copy(source, out.at[:, pl.ds(col * 2, 2)], orecv).start()

    for buf, k, slot in halos:
        drain(buf, k, slot)

    @pl.when(patch_self)
    def _():
        part = tin.at[:, 0:28]
        pltpu.make_async_copy(part, part, xsend).wait()

    @pl.when(jnp.logical_not(patch_self))
    def _():
        pltpu.make_async_copy(tin, tin, xsend).wait()

    part = sin.at[:, 0:30]
    pltpu.make_async_copy(part, part, rsend).wait()
    pltpu.make_async_copy(part, part, osend).wait()
    pltpu.make_async_copy(out, out, orecv).wait()


def on_device(tin, tw, sin, dw, pw, proj):
    anywhere = pl.BlockSpec(memory_space=pl.ANY)
    dma = pltpu.SemaphoreType.DMA

    def tile(k, c, kind):
        return pltpu.VMEM((TH + 2 * k, TW + 2 * k, 8, c), kind)

    scratch = [
        pltpu.VMEM((8, TH, 2, 8, CT), BF16),
        pltpu.VMEM((2, 512, CS), F32),
        tile(0, CT, F32),
        tile(1, CT, BF16),
        tile(1, CT, BF16),
        tile(1, WIDE, F32),
        pltpu.VMEM((512, 9 * WIDE), BF16),
        pltpu.VMEM((2, 3, 3, 3, WIDE, CT), BF16),
        pltpu.VMEM((3, 512, CT), F32),
        pltpu.VMEM((8, TH, 2, 8, CS), BF16),
        pltpu.VMEM((512, CS), F32),
        tile(2, CS, F32),
        tile(2, CS, F32),
        tile(2, CS, F32),
        tile(1, CS, F32),
        tile(1, CS, F32),
        tile(1, CS, F32),
        tile(0, CS, F32),
        tile(0, CS, F32),
        tile(0, CS, F32),
        tile(1, CS, F32),
        tile(2, CS, F32),
        tile(2, CS, BF16),
        tile(2, CS, BF16),
        tile(3, CS, BF16),
        tile(4, CS, BF16),
        tile(4, CS, F32),
        tile(4, CS, F32),
        tile(3, CS, F32),
        tile(2, CS, F32),
        pltpu.VMEM((512, CS), BF16),
        pltpu.VMEM((512, CT), BF16),
        pltpu.VMEM((512, CT), F32),
        pltpu.VMEM((8, TH, 2, 8, CS), BF16),
        pltpu.VMEM((3, 3, 3, 4, CS), F32),
        pltpu.VMEM((4, CS, CS), BF16),
        pltpu.VMEM((CT, CS), BF16),
        dma((9,)),
        dma(()),
        dma(()),
        dma(()),
        dma(()),
        dma(()),
        dma(()),
        dma((6, 8)),
        dma((6, 8)),
    ]
    result = pl.pallas_call(
        kernel,
        out_shape=jax.ShapeDtypeStruct((2, 32, 8, CS), BF16),
        in_specs=[anywhere] * 6,
        out_specs=anywhere,
        scratch_shapes=scratch,
        compiler_params=pltpu.CompilerParams(
            collective_id=0, has_side_effects=True, vmem_limit_bytes=56 * 1024 * 1024
        ),
    )(tin, tw, sin.reshape(2, 32, 8, CS), dw.transpose(1, 2, 3, 0, 4), pw, proj.T)
    return result.reshape(2, 1, 256, CS)


def solution(mesh):
    rows = P("ta", ("ha", "wa"), None, None)
    return jax.shard_map(
        on_device,
        mesh=mesh,
        in_specs=(P("ta", "ha", "wa", None), P(), rows, P(), P(), P()),
        out_specs=rows,
        check_vma=False,
    )
```

```python
import jax
import jax.numpy as jnp
from jax import lax
from jax.experimental import pallas as pl
from jax.experimental.pallas import tpu as pltpu
from jax.sharding import PartitionSpec as P

MESH = pl.DeviceIdType.MESH
F32, BF16 = jnp.float32, jnp.bfloat16
SIDES = [(-1, 0), (1, 0), (-1, -1), (-1, 1), (1, -1), (1, 1), (0, -1), (0, 1)]
FAR_FIRST = (2, 1, 3, 0)
CT, CS, WIDE = 192, 128, 256
TH, TW = 8, 8
GRID_R, GRID_C = 16, 32
TRANSPOSED = (((1,), (1,)), ((), ()))


def rational(x):
    gate = 0.5 * jnp.tanh(0.5 * x) + 0.5
    return x * gate


def act(s):
    gate = 0.5 * jnp.tanh(0.5 * s) + 0.5
    u = s * gate
    return u, gate + u * (1.0 - gate)


def silu_norm(x):
    scale = lax.rsqrt(jnp.sum(x * x, axis=-1, keepdims=True) * (1.0 / CT) + 1e-06)
    return rational(x * scale)


def shifted(v, by, frames):
    if by > 0:
        return jnp.where(frames >= by, pltpu.roll(v, by, v.ndim - 2), 0.0)
    return jnp.where(frames < 8 + by, pltpu.roll(v, 8 + by, v.ndim - 2), 0.0)


def kernel(
    tin, tw, sin, dw, pw, proj, out,
    xin, xf, xt, hact, hsec, af, lhs, wb, pp,
    rin, rf, s0f, s2f, u12, u10, d10, mm10, d8, mm8, sl0, sl1, sl2,
    h0, h2, hs, hg, gf, eb, g14, g12, s4b, mb, pr, ob, dwv, pwv, projv,
    wsem, xsend, xrecv, rsend, rrecv, osend, orecv, hsend, hrecv,
):
    ta, ha, wa = lax.axis_index("ta"), lax.axis_index("ha"), lax.axis_index("wa")
    z, low = lax.div(wa, 4), lax.rem(wa, 4)

    def bent(p):
        return jnp.where(p < 2, p, 5 - p)

    def place(c, a, b):
        p = bent(b)
        p = a * 4 + jnp.where(lax.rem(a, 2) == 0, p, 3 - p)
        return jnp.where(lax.rem(c, 2) == 0, p, 31 - p)

    row, col, line = ha * 4 + lax.div(z, 2), place(z, ta, low), lax.rem(wa, 8)

    def at(a, b, c):
        return {"ta": a, "ha": b, "wa": c}

    def owner(r, c):
        side = lax.div(c, 16)
        p = jnp.where(side == 0, c, 31 - c)
        a, p = lax.div(p, 4), lax.rem(p, 4)
        p = bent(jnp.where(lax.rem(a, 2) == 0, p, 3 - p))
        return at(a, lax.div(r, 4), lax.rem(r, 4) * 8 + side * 4 + p)

    neighbours = {side: owner(row + side[0], col + side[1]) for side in SIDES}
    fits_row = {-1: row > 0, 0: row >= 0, 1: row < GRID_R - 1}
    fits_col = {-1: col > 0, 0: col >= 0, 1: col < GRID_C - 1}
    present = {side: fits_row[side[0]] & fits_col[side[1]] for side in SIDES}

    def near(dr, dc):
        return neighbours[dr, dc]

    def there(dr, dc):
        return present[dr, dc]

    weights = []
    for b in range(2):
        for i in range(3):
            weights.append(
                pltpu.make_async_copy(
                    tw.at[0, b, i], wb.at[b, i, :, :, 0:CT, :], wsem.at[b * 3 + i]
                )
            )
    small = [
        pltpu.make_async_copy(dw, dwv, wsem.at[6]),
        pltpu.make_async_copy(pw, pwv, wsem.at[7]),
        pltpu.make_async_copy(proj, projv, wsem.at[8]),
    ]
    def clear_outside(buf, k):
        @pl.when(row == 0)
        def _():
            buf[0:k] = jnp.zeros_like(buf[0:k])

        @pl.when(row == GRID_R - 1)
        def _():
            buf[TH + k :] = jnp.zeros_like(buf[TH + k :])

        @pl.when(col == 0)
        def _():
            buf[:, 0:k] = jnp.zeros_like(buf[:, 0:k])

        @pl.when(col == GRID_C - 1)
        def _():
            buf[:, TW + k :] = jnp.zeros_like(buf[:, TW + k :])

    halos = ((hact, 1, 0), (h0, 2, 1), (hsec, 1, 2), (h2, 2, 3), (hs, 3, 4), (hg, 4, 5))
    for buf, k, _ in halos:
        clear_outside(buf, k)

    barrier = pltpu.get_barrier_semaphore()

    def greet(device):
        pl.semaphore_signal(barrier, inc=1, device_id=device, device_id_type=MESH)

    same = wa == col
    for step in range(4):
        r = ha * 4 + lax.rem(row + step, 4)
        if step:
            greet(owner(r, wa))
            greet(at(lax.rem(ta + step, 4), ha, col))
        else:
            @pl.when(jnp.logical_not(same))
            def _():
                greet(owner(r, wa))
                greet(at(ta, ha, col))

    @pl.loop(1, 32)
    def _(step):
        greet(owner(row, lax.rem(col + step, 32)))

    near_count = 0
    for dr, dc in SIDES:
        near_count = near_count + there(dr, dc).astype(jnp.int32)

        @pl.when(there(dr, dc))
        def _():
            greet(near(dr, dc))

    pl.semaphore_wait(barrier, 39 - 2 * same.astype(jnp.int32) + near_count)

    for step in FAR_FIRST:
        to = lax.rem(row + step, 4)
        source, target = tin.at[:, pl.ds(to * TH, TH)], xin.at[pl.ds(ta * 2, 2)]

        def send_patch():
            pltpu.make_async_remote_copy(
                src_ref=source,
                dst_ref=target,
                send_sem=xsend,
                recv_sem=xrecv,
                device_id=owner(ha * 4 + to, wa),
                device_id_type=MESH,
            ).start()

        if step:
            send_patch()
        else:
            @pl.when(same)
            def _():
                pltpu.make_async_copy(source, target, xrecv).start()

            pl.when(jnp.logical_not(same))(send_patch)

    pltpu.make_async_copy(sin.at[:, col], rin.at[pl.ds(ta * 2, 2), line], rrecv).start()

    @pl.loop(1, 32)
    def _(step):
        c = lax.rem(col + step, 32)
        pltpu.make_async_remote_copy(
            src_ref=sin.at[:, c],
            dst_ref=rin.at[pl.ds(ta * 2, 2), line],
            send_sem=rsend,
            recv_sem=rrecv,
            device_id=owner(row, c),
            device_id_type=MESH,
        ).start()

    for copy in small + weights:
        copy.start()
    af[:, :, :, CS:WIDE] = jnp.zeros((TH + 2, TW + 2, 8, WIDE - CS), F32)
    wb[:, :, :, :, CT:WIDE, :] = jnp.zeros((2, 3, 3, 3, WIDE - CT, CT), BF16)

    def side_copy(buf, k, slot, d):
        dr, dc = SIDES[d]

        def source(side, size):
            return pl.ds(*{-1: (k, k), 0: (k, size), 1: (size, k)}[side])

        def target(side, size):
            return pl.ds(*{-1: (size + k, k), 0: (k, size), 1: (0, k)}[side])

        return pltpu.make_async_remote_copy(
            src_ref=buf.at[source(dr, TH), source(dc, TW)],
            dst_ref=buf.at[target(dr, TH), target(dc, TW)],
            send_sem=hsend.at[slot, d],
            recv_sem=hrecv.at[slot, d],
            device_id=near(dr, dc),
            device_id_type=MESH,
        )

    def send(buf, k, slot):
        for d, (dr, dc) in enumerate(SIDES):
            @pl.when(there(dr, dc))
            def _():
                side_copy(buf, k, slot, d).start()

    def receive(buf, k, slot):
        for d, (dr, dc) in enumerate(SIDES):
            @pl.when(there(-dr, -dc))
            def _():
                side_copy(buf, k, slot, d).wait_recv()

    def drain(buf, k, slot):
        for d, (dr, dc) in enumerate(SIDES):
            @pl.when(there(dr, dc))
            def _():
                side_copy(buf, k, slot, d).wait_send()

    def ring(k):
        rows, cols = TH + 2 * k, TW + 2 * k
        return [
            (slice(0, k), slice(0, cols)),
            (slice(TH + k, rows), slice(0, cols)),
            (slice(k, TH + k), slice(0, k)),
            (slice(k, TH + k), slice(TW + k, cols)),
        ]

    frames = lax.broadcasted_iota(jnp.int32, (1, 8, CS), 1)
    wide_frames = lax.broadcasted_iota(jnp.int32, (1, 8, CT), 1)

    def taps(src, h, start, width, n, flip):
        acc = [None] * 3
        for j in range(3):
            for l in range(3):
                x = src[h + j, start + l : start + l + width]
                for i in range(3):
                    jj, ll = (2 - j, 2 - l) if flip else (j, l)
                    term = x * dwv[i, jj, ll, n : n + 1, :].reshape(1, 1, CS)
                    acc[i] = term if acc[i] is None else acc[i] + term
        sign = -1 if flip else 1
        return acc[2] + shifted(acc[1], sign, frames) + shifted(acc[0], 2 * sign, frames)

    def conv(b):
        for j in range(3):
            for l in range(3):
                at_lane = (j * 3 + l) * WIDE
                lhs[:, at_lane : at_lane + WIDE] = (
                    af[j : j + TH, l : l + TW].reshape(512, WIDE).astype(BF16)
                )
        for i in range(3):
            weights[b * 3 + i].wait()
            pp[i] = jnp.dot(
                lhs[...], wb[b, i].reshape(9 * WIDE, CT), preferred_element_type=F32
            )

    def conv_row(m):
        p = [pp[i, pl.ds(m * 64, 64)].reshape(8, 8, CT) for i in range(3)]
        return p[2] + shifted(p[1], 1, wide_frames) + shifted(p[0], 2, wide_frames)

    pltpu.make_async_copy(rin, rin, rrecv).wait()
    rf[...] = rin[...].astype(F32).reshape(512, CS)

    @pl.loop(0, TH)
    def _(h):
        for w in range(TW):
            s = rf[pl.ds(h * TW + w, 8, stride=64), :]
            s0f[h + 2, w + 2] = s
            h0[h + 2, w + 2] = s.astype(BF16)
            u, slope = act(s)
            u12[h + 2, w + 2] = u
            sl0[h, w] = slope

    send(h0, 2, 1)

    pltpu.make_async_copy(xin, xin, xrecv).wait()
    xall = xin[...].astype(F32).reshape(512, CT)
    xf[0] = xall[:, 0:CS]
    xf[1, :, 0 : CT - CS] = xall[:, CS:CT]

    @pl.loop(0, TH)
    def _(h):
        for w in range(TW):
            spot = pl.ds(h * TW + w, 8, stride=64)
            x = jnp.concatenate([xf[0, spot, :], xf[1, spot, :][:, 0 : CT - CS]], axis=-1)
            xt[h, w] = x
            a = silu_norm(x)
            hact[h + 1, w + 1] = a.astype(BF16)
            af[h + 1, w + 1, :, 0:CT] = a

    send(hact, 1, 0)

    for copy in small:
        copy.wait()

    def wide_layer(n, field):
        @pl.loop(0, TH + 2)
        def _(h):
            d10[h] = taps(u12, h, 0, 10, n, False)

        mm10[...] = jnp.dot(
            d10[...].reshape(800, CS).astype(BF16), pwv[n], preferred_element_type=F32
        ).reshape(10, 10, 8, CS)

        @pl.loop(0, TH + 2)
        def _(h):
            s = field[h + 1, 1:11] + mm10[h]
            mm10[h] = s
            u, slope = act(s)
            u10[h] = u
            sl1[h] = slope

        clear_outside(u10, 1)

    def narrow_layer(n):
        @pl.loop(0, TH)
        def _(h):
            d8[h] = taps(u10, h, 0, 8, n, False)

        mm8[...] = jnp.dot(
            d8[...].reshape(512, CS).astype(BF16), pwv[n], preferred_element_type=F32
        ).reshape(8, 8, 8, CS)

    receive(h0, 2, 1)
    for rows, cols in ring(2):
        s = h0[rows, cols].astype(F32)
        s0f[rows, cols] = s
        u12[rows, cols] = act(s)[0]
    wide_layer(0, s0f)
    narrow_layer(1)

    @pl.loop(0, TH)
    def _(h):
        s = mm10[h + 1, 1:9] + mm8[h]
        s2f[h + 2, 2:10] = s
        h2[h + 2, 2:10] = s.astype(BF16)
        u, slope = act(s)
        u12[h + 2, 2:10] = u
        sl2[h + 2, 2:10] = slope

    send(h2, 2, 3)

    receive(hact, 1, 0)
    for rows, cols in ring(1):
        af[rows, cols, :, 0:CT] = hact[rows, cols].astype(F32)
    conv(0)

    @pl.loop(0, 8)
    def _(m):
        a = silu_norm(conv_row(m))
        hsec[m + 1, 1:9] = a.astype(BF16)
        af[m + 1, 1:9, :, 0:CT] = a

    send(hsec, 1, 2)

    receive(h2, 2, 3)
    for rows, cols in ring(2):
        s = h2[rows, cols].astype(F32)
        s2f[rows, cols] = s
        u, slope = act(s)
        u12[rows, cols] = u
        sl2[rows, cols] = slope

    @pl.loop(0, TH + 2)
    def _(h):
        d10[h] = taps(u12, h, 0, 10, 2, False)

    mm10[...] = jnp.dot(
        d10[...].reshape(800, CS).astype(BF16), pwv[2], preferred_element_type=F32
    ).reshape(10, 10, 8, CS)

    @pl.loop(0, TH + 2)
    def _(h):
        s = s2f[h + 1, 1:11] + mm10[h]
        mm10[h] = s
        u, slope = act(s)
        u10[h] = u
        d10[h] = slope

    hs[3:11, 3:11] = d10[1:9, 1:9].astype(BF16)
    send(hs, 3, 4)
    clear_outside(u10, 1)
    narrow_layer(3)
    s4b[...] = (mm10[1:9, 1:9] + mm8[...]).reshape(512, CS).astype(BF16)

    pr[...] = lax.dot_general(s4b[...], projv[...], TRANSPOSED, preferred_element_type=F32)

    receive(hsec, 1, 2)
    for rows, cols in ring(1):
        af[rows, cols, :, 0:CT] = hsec[rows, cols].astype(F32)
    conv(1)

    @pl.loop(0, 8)
    def _(m):
        target = (xt[m] + conv_row(m)).reshape(64, CT)
        span = pl.ds(m * 64, 64)
        mb[span] = (pr[span] - target).astype(BF16)

    g = jnp.dot(mb[...], projv[...], preferred_element_type=F32).reshape(8, 8, 8, CS)
    gf[4:12, 4:12] = g
    hg[4:12, 4:12] = g.astype(BF16)
    send(hg, 4, 5)

    receive(hs, 3, 4)
    receive(hg, 4, 5)
    for rows, cols in ring(4):
        gf[rows, cols] = hg[rows, cols].astype(F32)

    def back(n, source, k):
        rows, cols = TH + 2 * k, TW + 2 * k
        eb[0:rows, 0:cols] = lax.dot_general(
            source[...].reshape(rows * cols * 8, CS).astype(BF16),
            pwv[n],
            TRANSPOSED,
            preferred_element_type=F32,
        ).reshape(rows, cols, 8, CS)

    back(3, gf, 4)

    @pl.loop(0, 14)
    def _(h):
        for w in (0, 7):
            slope = hs[h, w : w + 7].astype(F32)
            g14[h, w : w + 7] = (
                gf[h + 1, w + 1 : w + 8] + taps(eb, h, w, 7, 3, True) * slope
            )

    clear_outside(g14, 3)
    back(2, g14, 3)

    @pl.loop(0, 12)
    def _(h):
        for w in (0, 6):
            g12[h, w : w + 6] = (
                g14[h + 1, w + 1 : w + 7]
                + taps(eb, h, w, 6, 2, True) * sl2[h, w : w + 6]
            )

    clear_outside(g12, 2)
    back(1, g12, 2)

    @pl.loop(0, 10)
    def _(h):
        d10[h] = g12[h + 1, 1:11] + taps(eb, h, 0, 10, 1, True) * sl1[h]

    clear_outside(d10, 1)
    back(0, d10, 1)

    def send_back(x, h):
        pltpu.make_async_remote_copy(
            src_ref=ob.at[pl.ds(x * 2, 2), h],
            dst_ref=out.at[:, col],
            send_sem=osend,
            recv_sem=orecv,
            device_id=at(x, ha, wa - line + h),
            device_id_type=MESH,
        ).start()

    @pl.loop(0, TH)
    def _(h):
        g = d10[h + 1, 1:9] + taps(eb, h, 0, 8, 0, True) * sl0[h]
        rf[pl.ds(h * 64, 64)] = g.reshape(64, CS)
        for t in range(8):
            ob[t, h] = rf[pl.ds(h * 64 + t, 8, stride=8), :].astype(BF16)
        for step in (2, 1, 3):
            send_back(lax.rem(ta + step, 4), h)

        @pl.when(h == line)
        def _():
            pltpu.make_async_copy(
                ob.at[pl.ds(ta * 2, 2), h], out.at[:, col], orecv
            ).start()

        @pl.when(h != line)
        def _():
            send_back(ta, h)

    for buf, k, slot in halos:
        drain(buf, k, slot)

    @pl.when(same)
    def _():
        part = tin.at[:, 0:24]
        pltpu.make_async_copy(part, part, xsend).wait()

    @pl.when(jnp.logical_not(same))
    def _():
        pltpu.make_async_copy(tin, tin, xsend).wait()

    part = sin.at[:, 0:31]
    pltpu.make_async_copy(part, part, rsend).wait()
    pltpu.make_async_copy(part, part, osend).wait()
    pltpu.make_async_copy(out, out, orecv).wait()


def on_device(tin, tw, sin, dw, pw, proj):
    anywhere = pl.BlockSpec(memory_space=pl.ANY)
    dma = pltpu.SemaphoreType.DMA

    def tile(k, c, kind):
        return pltpu.VMEM((TH + 2 * k, TW + 2 * k, 8, c), kind)

    scratch = [
        pltpu.VMEM((8, 8, 8, CT), BF16),
        pltpu.VMEM((2, 512, CS), F32),
        tile(0, CT, F32),
        tile(1, CT, BF16),
        tile(1, CT, BF16),
        tile(1, WIDE, F32),
        pltpu.VMEM((512, 9 * WIDE), BF16),
        pltpu.VMEM((2, 3, 3, 3, WIDE, CT), BF16),
        pltpu.VMEM((3, 512, CT), F32),
        pltpu.VMEM((8, 8, 8, CS), BF16),
        pltpu.VMEM((512, CS), F32),
        tile(2, CS, F32),
        tile(2, CS, F32),
        tile(2, CS, F32),
        tile(1, CS, F32),
        tile(1, CS, F32),
        tile(1, CS, F32),
        tile(0, CS, F32),
        tile(0, CS, F32),
        tile(0, CS, F32),
        tile(1, CS, F32),
        tile(2, CS, F32),
        tile(2, CS, BF16),
        tile(2, CS, BF16),
        tile(3, CS, BF16),
        tile(4, CS, BF16),
        tile(4, CS, F32),
        tile(4, CS, F32),
        tile(3, CS, F32),
        tile(2, CS, F32),
        pltpu.VMEM((512, CS), BF16),
        pltpu.VMEM((512, CT), BF16),
        pltpu.VMEM((512, CT), F32),
        pltpu.VMEM((8, 8, 8, CS), BF16),
        pltpu.VMEM((3, 3, 3, 4, CS), F32),
        pltpu.VMEM((4, CS, CS), BF16),
        pltpu.VMEM((CT, CS), BF16),
        dma((9,)),
        dma(()),
        dma(()),
        dma(()),
        dma(()),
        dma(()),
        dma(()),
        dma((6, 8)),
        dma((6, 8)),
    ]
    result = pl.pallas_call(
        kernel,
        out_shape=jax.ShapeDtypeStruct((2, 32, 8, CS), BF16),
        in_specs=[anywhere] * 6,
        out_specs=anywhere,
        scratch_shapes=scratch,
        compiler_params=pltpu.CompilerParams(
            collective_id=0, has_side_effects=True, vmem_limit_bytes=56 * 1024 * 1024
        ),
    )(tin, tw, sin.reshape(2, 32, 8, CS), dw.transpose(1, 2, 3, 0, 4), pw, proj.T)
    return result.reshape(2, 1, 256, CS)


def solution(mesh):
    rows = P("ta", ("ha", "wa"), None, None)
    return jax.shard_map(
        on_device,
        mesh=mesh,
        in_specs=(P("ta", "ha", "wa", None), P(), rows, P(), P(), P()),
        out_specs=rows,
        check_vma=False,
    )
```

```python
import jax
import jax.numpy as jnp
from jax import lax
from jax.experimental import pallas as pl
from jax.experimental.pallas import tpu as pltpu
from jax.sharding import PartitionSpec as P

MESH = pl.DeviceIdType.MESH
F32, BF16 = jnp.float32, jnp.bfloat16
SIDES = [(-1, 0), (1, 0), (-1, -1), (-1, 1), (1, -1), (1, 1), (0, -1), (0, 1)]
FAR_FIRST = (4, 3, 5, 2, 6, 1, 7, 0)
CT, CS, WIDE = 192, 128, 256
TH, TW = 4, 16
GRID_R, GRID_C = 32, 16
TRANSPOSED = (((1,), (1,)), ((), ()))


def rational(x):
    gate = 0.5 * jnp.tanh(0.5 * x) + 0.5
    return x * gate


def act(s):
    gate = 0.5 * jnp.tanh(0.5 * s) + 0.5
    u = s * gate
    return u, gate + u * (1.0 - gate)


def silu_norm(x):
    scale = lax.rsqrt(jnp.sum(x * x, axis=-1, keepdims=True) * (1.0 / CT) + 1e-06)
    return rational(x * scale)


def shifted(v, by, frames):
    if by > 0:
        return jnp.where(frames >= by, pltpu.roll(v, by, v.ndim - 2), 0.0)
    return jnp.where(frames < 8 + by, pltpu.roll(v, 8 + by, v.ndim - 2), 0.0)


def kernel(
    tin, tw, sin, dw, pw, proj, out,
    xin, xf, xt, hact, hsec, af, lhs, wb, pp,
    rin, rf, s0f, s2f, u20, u18, d18, mm18, d16, mm16, sl0, sl1, sl2,
    h0, h2, hs, hg, gf, eb, g22, g20, s4b, mb, pr, ob, dwv, pwv, projv,
    wsem, xsend, xrecv, rsend, rrecv, osend, orecv, hsend, hrecv,
):
    ta, ha, wa = lax.axis_index("ta"), lax.axis_index("ha"), lax.axis_index("wa")
    z, low = lax.div(wa, 4), lax.rem(wa, 4)

    def bent(p):
        return jnp.where(p < 2, p, 5 - p)

    def place(a, b):
        p = bent(b)
        return a * 4 + jnp.where(lax.rem(a, 2) == 0, p, 3 - p)

    upper = lax.div(low, 2)
    spot, col = lax.rem(z + 8 - upper, 8), place(ta, low)
    row, held = ha * 8 + spot, ha * 8 + z
    first = upper == 0

    def at(a, b, c):
        return {"ta": a, "ha": b, "wa": c}

    def owner(r, c):
        a, p = lax.div(c, 4), lax.rem(c, 4)
        p = bent(jnp.where(lax.rem(a, 2) == 0, p, 3 - p))
        return at(a, lax.div(r, 8), lax.rem(lax.rem(r, 8) + lax.div(p, 2), 8) * 4 + p)

    neighbours = {side: owner(row + side[0], col + side[1]) for side in SIDES}
    fits_row = {-1: row > 0, 0: row >= 0, 1: row < GRID_R - 1}
    fits_col = {-1: col > 0, 0: col >= 0, 1: col < GRID_C - 1}
    present = {side: fits_row[side[0]] & fits_col[side[1]] for side in SIDES}

    def near(dr, dc):
        return neighbours[dr, dc]

    def there(dr, dc):
        return present[dr, dc]

    weights = []
    for b in range(2):
        for i in range(3):
            weights.append(
                pltpu.make_async_copy(
                    tw.at[0, b, i], wb.at[b, i, :, :, 0:CT, :], wsem.at[b * 3 + i]
                )
            )
    small = [
        pltpu.make_async_copy(dw, dwv, wsem.at[6]),
        pltpu.make_async_copy(pw, pwv, wsem.at[7]),
        pltpu.make_async_copy(proj, projv, wsem.at[8]),
    ]
    def clear_outside(buf, k):
        @pl.when(row == 0)
        def _():
            buf[0:k] = jnp.zeros_like(buf[0:k])

        @pl.when(row == GRID_R - 1)
        def _():
            buf[TH + k :] = jnp.zeros_like(buf[TH + k :])

        @pl.when(col == 0)
        def _():
            buf[:, 0:k] = jnp.zeros_like(buf[:, 0:k])

        @pl.when(col == GRID_C - 1)
        def _():
            buf[:, TW + k :] = jnp.zeros_like(buf[:, TW + k :])

    halos = ((hact, 1, 0), (h0, 2, 1), (hsec, 1, 2), (h2, 2, 3), (hs, 3, 4), (hg, 4, 5))
    for buf, k, _ in halos:
        clear_outside(buf, k)

    barrier = pltpu.get_barrier_semaphore()

    def greet(device):
        pl.semaphore_signal(barrier, inc=1, device_id=device, device_id_type=MESH)

    block = lax.div(wa, 2)
    same = block == col

    @pl.loop(0, 8)
    def _(step):
        r = ha * 8 + lax.rem(spot + step, 8)

        @pl.when(jnp.logical_not((step == 0) & same))
        def _():
            greet(owner(r, block))

        a, b = lax.div(step, 2), 2 * col + lax.rem(step, 2)

        @pl.when(jnp.logical_not((a == ta) & (b == wa)))
        def _():
            greet(at(a, ha, b))

    @pl.loop(0, 16)
    def _(step):
        @pl.when(jnp.logical_not(first & (step == 0)))
        def _():
            greet(owner(held, lax.rem(col + step, 16)))

        x, y = lax.div(step, 4), lax.rem(step, 4)

        @pl.when(jnp.logical_not(first & (x == ta) & (y == low)))
        def _():
            greet(at(x, ha, spot * 4 + y))

    near_count = 0
    for dr, dc in SIDES:
        near_count = near_count + there(dr, dc).astype(jnp.int32)

        @pl.when(there(dr, dc))
        def _():
            greet(near(dr, dc))

    pl.semaphore_wait(
        barrier, 48 - 2 * same.astype(jnp.int32) - 2 * first.astype(jnp.int32) + near_count
    )

    for step in FAR_FIRST:
        to = lax.rem(spot + step, 8)
        source = tin.at[:, pl.ds(to * TH, TH)]
        target = xin.at[pl.ds(ta * 2, 2), :, lax.rem(wa, 2)]

        def send_patch():
            pltpu.make_async_remote_copy(
                src_ref=source,
                dst_ref=target,
                send_sem=xsend,
                recv_sem=xrecv,
                device_id=owner(ha * 8 + to, block),
                device_id_type=MESH,
            ).start()

        if step:
            send_patch()
        else:
            @pl.when(same)
            def _():
                pltpu.make_async_copy(source, target, xrecv).start()

            pl.when(jnp.logical_not(same))(send_patch)

    @pl.loop(0, 16)
    def _(step):
        c = lax.rem(col + step, 16)
        source, target = sin.at[:, pl.ds(c * 2, 2)], rin.at[pl.ds(ta * 2, 2), low]
        itself = first & (step == 0)

        @pl.when(itself)
        def _():
            pltpu.make_async_copy(source, target, rrecv).start()

        @pl.when(jnp.logical_not(itself))
        def _():
            pltpu.make_async_remote_copy(
                src_ref=source,
                dst_ref=target,
                send_sem=rsend,
                recv_sem=rrecv,
                device_id=owner(held, c),
                device_id_type=MESH,
            ).start()

    for copy in small + weights:
        copy.start()
    af[:, :, :, CS:WIDE] = jnp.zeros((TH + 2, TW + 2, 8, WIDE - CS), F32)
    wb[:, :, :, :, CT:WIDE, :] = jnp.zeros((2, 3, 3, 3, WIDE - CT, CT), BF16)

    def side_copy(buf, k, slot, d):
        dr, dc = SIDES[d]

        def source(side, size):
            return pl.ds(*{-1: (k, k), 0: (k, size), 1: (size, k)}[side])

        def target(side, size):
            return pl.ds(*{-1: (size + k, k), 0: (k, size), 1: (0, k)}[side])

        return pltpu.make_async_remote_copy(
            src_ref=buf.at[source(dr, TH), source(dc, TW)],
            dst_ref=buf.at[target(dr, TH), target(dc, TW)],
            send_sem=hsend.at[slot, d],
            recv_sem=hrecv.at[slot, d],
            device_id=near(dr, dc),
            device_id_type=MESH,
        )

    def send(buf, k, slot):
        for d, (dr, dc) in enumerate(SIDES):
            @pl.when(there(dr, dc))
            def _():
                side_copy(buf, k, slot, d).start()

    def receive(buf, k, slot):
        for d, (dr, dc) in enumerate(SIDES):
            @pl.when(there(-dr, -dc))
            def _():
                side_copy(buf, k, slot, d).wait_recv()

    def drain(buf, k, slot):
        for d, (dr, dc) in enumerate(SIDES):
            @pl.when(there(dr, dc))
            def _():
                side_copy(buf, k, slot, d).wait_send()

    def ring(k):
        rows, cols = TH + 2 * k, TW + 2 * k
        return [
            (slice(0, k), slice(0, cols)),
            (slice(TH + k, rows), slice(0, cols)),
            (slice(k, TH + k), slice(0, k)),
            (slice(k, TH + k), slice(TW + k, cols)),
        ]

    frames = lax.broadcasted_iota(jnp.int32, (1, 8, CS), 1)
    wide_frames = lax.broadcasted_iota(jnp.int32, (1, 8, CT), 1)

    def taps(src, h, start, width, n, flip):
        acc = [None] * 3
        for j in range(3):
            for l in range(3):
                x = src[h + j, start + l : start + l + width]
                for i in range(3):
                    jj, ll = (2 - j, 2 - l) if flip else (j, l)
                    term = x * dwv[i, jj, ll, n : n + 1, :].reshape(1, 1, CS)
                    acc[i] = term if acc[i] is None else acc[i] + term
        sign = -1 if flip else 1
        return acc[2] + shifted(acc[1], sign, frames) + shifted(acc[0], 2 * sign, frames)

    def conv(b):
        for j in range(3):
            for l in range(3):
                at_lane = (j * 3 + l) * WIDE
                lhs[:, at_lane : at_lane + WIDE] = (
                    af[j : j + TH, l : l + TW].reshape(512, WIDE).astype(BF16)
                )
        for i in range(3):
            weights[b * 3 + i].wait()
            pp[i] = jnp.dot(
                lhs[...], wb[b, i].reshape(9 * WIDE, CT), preferred_element_type=F32
            )

    def conv_row(m):
        p = [pp[i, pl.ds(m * 64, 64)].reshape(8, 8, CT) for i in range(3)]
        return p[2] + shifted(p[1], 1, wide_frames) + shifted(p[0], 2, wide_frames)

    pltpu.make_async_copy(rin, rin, rrecv).wait()
    rf[...] = rin[...].astype(F32).reshape(512, CS)

    @pl.loop(0, TH)
    def _(h):
        for w in range(TW):
            s = rf[pl.ds(h * TW + w, 8, stride=64), :]
            s0f[h + 2, w + 2] = s
            h0[h + 2, w + 2] = s.astype(BF16)
            u, slope = act(s)
            u20[h + 2, w + 2] = u
            sl0[h, w] = slope

    send(h0, 2, 1)

    pltpu.make_async_copy(xin, xin, xrecv).wait()
    xall = xin[...].astype(F32).reshape(512, CT)
    xf[0] = xall[:, 0:CS]
    xf[1, :, 0 : CT - CS] = xall[:, CS:CT]

    @pl.loop(0, TH)
    def _(h):
        for w in range(TW):
            spot = pl.ds(h * TW + w, 8, stride=64)
            x = jnp.concatenate([xf[0, spot, :], xf[1, spot, :][:, 0 : CT - CS]], axis=-1)
            xt[h, w] = x
            a = silu_norm(x)
            hact[h + 1, w + 1] = a.astype(BF16)
            af[h + 1, w + 1, :, 0:CT] = a

    send(hact, 1, 0)

    for copy in small:
        copy.wait()

    def wide_layer(n, field):
        @pl.loop(0, TH + 2)
        def _(h):
            for w in (0, 9):
                d18[h, w : w + 9] = taps(u20, h, w, 9, n, False)

        mm18[...] = jnp.dot(
            d18[...].reshape(864, CS).astype(BF16), pwv[n], preferred_element_type=F32
        ).reshape(6, 18, 8, CS)

        @pl.loop(0, TH + 2)
        def _(h):
            s = field[h + 1, 1:19] + mm18[h]
            mm18[h] = s
            u, slope = act(s)
            u18[h] = u
            sl1[h] = slope

        clear_outside(u18, 1)

    def narrow_layer(n):
        @pl.loop(0, TH)
        def _(h):
            for w in (0, 8):
                d16[h, w : w + 8] = taps(u18, h, w, 8, n, False)

        mm16[...] = jnp.dot(
            d16[...].reshape(512, CS).astype(BF16), pwv[n], preferred_element_type=F32
        ).reshape(4, 16, 8, CS)

    receive(h0, 2, 1)
    for rows, cols in ring(2):
        s = h0[rows, cols].astype(F32)
        s0f[rows, cols] = s
        u20[rows, cols] = act(s)[0]
    wide_layer(0, s0f)
    narrow_layer(1)

    @pl.loop(0, TH)
    def _(h):
        s = mm18[h + 1, 1:17] + mm16[h]
        s2f[h + 2, 2:18] = s
        h2[h + 2, 2:18] = s.astype(BF16)
        u, slope = act(s)
        u20[h + 2, 2:18] = u
        sl2[h + 2, 2:18] = slope

    send(h2, 2, 3)

    receive(hact, 1, 0)
    for rows, cols in ring(1):
        af[rows, cols, :, 0:CT] = hact[rows, cols].astype(F32)
    conv(0)

    @pl.loop(0, 8)
    def _(m):
        h, w = lax.div(m, 2), lax.rem(m, 2) * 8
        a = silu_norm(conv_row(m))
        hsec[h + 1, pl.ds(w + 1, 8)] = a.astype(BF16)
        af[h + 1, pl.ds(w + 1, 8), :, 0:CT] = a

    send(hsec, 1, 2)

    receive(h2, 2, 3)
    for rows, cols in ring(2):
        s = h2[rows, cols].astype(F32)
        s2f[rows, cols] = s
        u, slope = act(s)
        u20[rows, cols] = u
        sl2[rows, cols] = slope

    @pl.loop(0, TH + 2)
    def _(h):
        for w in (0, 9):
            d18[h, w : w + 9] = taps(u20, h, w, 9, 2, False)

    mm18[...] = jnp.dot(
        d18[...].reshape(864, CS).astype(BF16), pwv[2], preferred_element_type=F32
    ).reshape(6, 18, 8, CS)

    @pl.loop(0, TH + 2)
    def _(h):
        s = s2f[h + 1, 1:19] + mm18[h]
        mm18[h] = s
        u, slope = act(s)
        u18[h] = u
        d18[h] = slope

    hs[3:7, 3:19] = d18[1:5, 1:17].astype(BF16)
    send(hs, 3, 4)
    clear_outside(u18, 1)
    narrow_layer(3)
    s4b[...] = (mm18[1:5, 1:17] + mm16[...]).reshape(512, CS).astype(BF16)

    pr[...] = lax.dot_general(s4b[...], projv[...], TRANSPOSED, preferred_element_type=F32)

    receive(hsec, 1, 2)
    for rows, cols in ring(1):
        af[rows, cols, :, 0:CT] = hsec[rows, cols].astype(F32)
    conv(1)

    @pl.loop(0, 8)
    def _(m):
        h, w = lax.div(m, 2), lax.rem(m, 2) * 8
        target = (xt[h, pl.ds(w, 8)] + conv_row(m)).reshape(64, CT)
        span = pl.ds(m * 64, 64)
        mb[span] = (pr[span] - target).astype(BF16)

    g = jnp.dot(mb[...], projv[...], preferred_element_type=F32).reshape(4, 16, 8, CS)
    gf[4:8, 4:20] = g
    hg[4:8, 4:20] = g.astype(BF16)
    send(hg, 4, 5)

    receive(hs, 3, 4)
    receive(hg, 4, 5)
    for rows, cols in ring(4):
        gf[rows, cols] = hg[rows, cols].astype(F32)

    def back(n, source, k):
        rows, cols = TH + 2 * k, TW + 2 * k
        eb[0:rows, 0:cols] = lax.dot_general(
            source[...].reshape(rows * cols * 8, CS).astype(BF16),
            pwv[n],
            TRANSPOSED,
            preferred_element_type=F32,
        ).reshape(rows, cols, 8, CS)

    back(3, gf, 4)

    @pl.loop(0, 10)
    def _(h):
        for w in (0, 11):
            slope = hs[h, w : w + 11].astype(F32)
            g22[h, w : w + 11] = (
                gf[h + 1, w + 1 : w + 12] + taps(eb, h, w, 11, 3, True) * slope
            )

    clear_outside(g22, 3)
    back(2, g22, 3)

    @pl.loop(0, 8)
    def _(h):
        for w in (0, 10):
            g20[h, w : w + 10] = (
                g22[h + 1, w + 1 : w + 11]
                + taps(eb, h, w, 10, 2, True) * sl2[h, w : w + 10]
            )

    clear_outside(g20, 2)
    back(1, g20, 2)

    @pl.loop(0, 6)
    def _(h):
        for w in (0, 9):
            d18[h, w : w + 9] = (
                g20[h + 1, w + 1 : w + 10]
                + taps(eb, h, w, 9, 1, True) * sl1[h, w : w + 9]
            )

    clear_outside(d18, 1)
    back(0, d18, 1)

    def send_back(x, h):
        pltpu.make_async_remote_copy(
            src_ref=ob.at[pl.ds(x * 2, 2), h],
            dst_ref=out.at[:, pl.ds(col * 2, 2)],
            send_sem=osend,
            recv_sem=orecv,
            device_id=at(x, ha, spot * 4 + h),
            device_id_type=MESH,
        ).start()

    @pl.loop(0, TH)
    def _(h):
        for w in (0, 8):
            g = (
                d18[h + 1, w + 1 : w + 9]
                + taps(eb, h, w, 8, 0, True) * sl0[h, w : w + 8]
            )
            rf[pl.ds(h * 128 + w * 8, 64)] = g.reshape(64, CS)
        for half in range(2):
            for t in range(8):
                ob[t, h, half] = rf[
                    pl.ds(h * 128 + half * 64 + t, 8, stride=8), :
                ].astype(BF16)
        for step in (2, 1, 3):
            send_back(lax.rem(ta + step, 4), h)

        @pl.when(first & (h == low))
        def _():
            pltpu.make_async_copy(
                ob.at[pl.ds(ta * 2, 2), h], out.at[:, pl.ds(col * 2, 2)], orecv
            ).start()

        @pl.when(jnp.logical_not(first & (h == low)))
        def _():
            send_back(ta, h)

    for buf, k, slot in halos:
        drain(buf, k, slot)

    @pl.when(same)
    def _():
        part = tin.at[:, 0:28]
        pltpu.make_async_copy(part, part, xsend).wait()

    @pl.when(jnp.logical_not(same))
    def _():
        pltpu.make_async_copy(tin, tin, xsend).wait()

    for sem in (rsend, osend):
        @pl.when(first)
        def _():
            part = sin.at[:, 0:30]
            pltpu.make_async_copy(part, part, sem).wait()

        @pl.when(jnp.logical_not(first))
        def _():
            pltpu.make_async_copy(sin, sin, sem).wait()

    pltpu.make_async_copy(out, out, orecv).wait()


def on_device(tin, tw, sin, dw, pw, proj):
    anywhere = pl.BlockSpec(memory_space=pl.ANY)
    dma = pltpu.SemaphoreType.DMA

    def tile(k, c, kind):
        return pltpu.VMEM((TH + 2 * k, TW + 2 * k, 8, c), kind)

    scratch = [
        pltpu.VMEM((8, TH, 2, 8, CT), BF16),
        pltpu.VMEM((2, 512, CS), F32),
        tile(0, CT, F32),
        tile(1, CT, BF16),
        tile(1, CT, BF16),
        tile(1, WIDE, F32),
        pltpu.VMEM((512, 9 * WIDE), BF16),
        pltpu.VMEM((2, 3, 3, 3, WIDE, CT), BF16),
        pltpu.VMEM((3, 512, CT), F32),
        pltpu.VMEM((8, TH, 2, 8, CS), BF16),
        pltpu.VMEM((512, CS), F32),
        tile(2, CS, F32),
        tile(2, CS, F32),
        tile(2, CS, F32),
        tile(1, CS, F32),
        tile(1, CS, F32),
        tile(1, CS, F32),
        tile(0, CS, F32),
        tile(0, CS, F32),
        tile(0, CS, F32),
        tile(1, CS, F32),
        tile(2, CS, F32),
        tile(2, CS, BF16),
        tile(2, CS, BF16),
        tile(3, CS, BF16),
        tile(4, CS, BF16),
        tile(4, CS, F32),
        tile(4, CS, F32),
        tile(3, CS, F32),
        tile(2, CS, F32),
        pltpu.VMEM((512, CS), BF16),
        pltpu.VMEM((512, CT), BF16),
        pltpu.VMEM((512, CT), F32),
        pltpu.VMEM((8, TH, 2, 8, CS), BF16),
        pltpu.VMEM((3, 3, 3, 4, CS), F32),
        pltpu.VMEM((4, CS, CS), BF16),
        pltpu.VMEM((CT, CS), BF16),
        dma((9,)),
        dma(()),
        dma(()),
        dma(()),
        dma(()),
        dma(()),
        dma(()),
        dma((6, 8)),
        dma((6, 8)),
    ]
    result = pl.pallas_call(
        kernel,
        out_shape=jax.ShapeDtypeStruct((2, 32, 8, CS), BF16),
        in_specs=[anywhere] * 6,
        out_specs=anywhere,
        scratch_shapes=scratch,
        compiler_params=pltpu.CompilerParams(
            collective_id=0, has_side_effects=True, vmem_limit_bytes=56 * 1024 * 1024
        ),
    )(tin, tw, sin.reshape(2, 32, 8, CS), dw.transpose(1, 2, 3, 0, 4), pw, proj.T)
    return result.reshape(2, 1, 256, CS)


def solution(mesh):
    rows = P("ta", ("ha", "wa"), None, None)
    return jax.shard_map(
        on_device,
        mesh=mesh,
        in_specs=(P("ta", "ha", "wa", None), P(), rows, P(), P(), P()),
        out_specs=rows,
        check_vma=False,
    )
```

```python
import jax
import jax.numpy as jnp
from jax import lax
from jax.experimental import pallas as pl
from jax.experimental.pallas import tpu as pltpu
from jax.sharding import PartitionSpec as P

MESH = pl.DeviceIdType.MESH
F32, BF16 = jnp.float32, jnp.bfloat16
SIDES = [(-1, 0), (1, 0), (-1, -1), (-1, 1), (1, -1), (1, 1), (0, -1), (0, 1)]
FAR_FIRST = (4, 3, 5, 2, 6, 1, 7, 0)
CT, CS, WIDE = 192, 128, 256
TH, TW = 4, 16
GRID_R, GRID_C = 32, 16
TRANSPOSED = (((1,), (1,)), ((), ()))


def rational(x):
    gate = 0.5 * jnp.tanh(0.5 * x) + 0.5
    return x * gate


def act(s):
    gate = 0.5 * jnp.tanh(0.5 * s) + 0.5
    u = s * gate
    return u, gate + u * (1.0 - gate)


def silu_norm(x):
    scale = lax.rsqrt(jnp.sum(x * x, axis=-1, keepdims=True) * (1.0 / CT) + 1e-06)
    return rational(x * scale)


def shifted(v, by, frames):
    if by > 0:
        return jnp.where(frames >= by, pltpu.roll(v, by, v.ndim - 2), 0.0)
    return jnp.where(frames < 8 + by, pltpu.roll(v, 8 + by, v.ndim - 2), 0.0)


def kernel(
    tin, tw, sin, dw, pw, proj, out,
    xin, xf, xt, hact, hsec, af, lhs, wb, pp,
    rin, rf, s0f, s2f, u20, u18, d18, mm18, d16, mm16, sl0, sl1, sl2,
    h0, h2, hs, hg, gf, eb, pa, pb, kb, g22, g20, s4b, mb, pr, ob, dwv, pwv, projv,
    wsem, xsend, xrecv, rsend, rrecv, osend, orecv, hsend, hrecv,
):
    ta, ha, wa = lax.axis_index("ta"), lax.axis_index("ha"), lax.axis_index("wa")
    z, low = lax.div(wa, 4), lax.rem(wa, 4)

    def bent(p):
        return jnp.where(p < 2, p, 5 - p)

    def place(a, b):
        p = bent(b)
        return a * 4 + jnp.where(lax.rem(a, 2) == 0, p, 3 - p)

    upper = lax.div(low, 2)
    spot, col = lax.rem(z + 8 - upper, 8), place(ta, low)
    row, held = ha * 8 + spot, ha * 8 + z
    first = upper == 0

    def at(a, b, c):
        return {"ta": a, "ha": b, "wa": c}

    def owner(r, c):
        a, p = lax.div(c, 4), lax.rem(c, 4)
        p = bent(jnp.where(lax.rem(a, 2) == 0, p, 3 - p))
        return at(a, lax.div(r, 8), lax.rem(lax.rem(r, 8) + lax.div(p, 2), 8) * 4 + p)

    neighbours = {side: owner(row + side[0], col + side[1]) for side in SIDES}
    fits_row = {-1: row > 0, 0: row >= 0, 1: row < GRID_R - 1}
    fits_col = {-1: col > 0, 0: col >= 0, 1: col < GRID_C - 1}
    present = {side: fits_row[side[0]] & fits_col[side[1]] for side in SIDES}

    def near(dr, dc):
        return neighbours[dr, dc]

    def there(dr, dc):
        return present[dr, dc]

    weights = []
    for b in range(2):
        for i in range(3):
            weights.append(
                pltpu.make_async_copy(
                    tw.at[0, b, i], wb.at[b, i, :, :, 0:CT, :], wsem.at[b * 3 + i]
                )
            )
    small = [
        pltpu.make_async_copy(dw, dwv, wsem.at[6]),
        pltpu.make_async_copy(pw, pwv, wsem.at[7]),
        pltpu.make_async_copy(proj, projv, wsem.at[8]),
    ]
    def clear_outside(buf, k):
        @pl.when(row == 0)
        def _():
            buf[0:k] = jnp.zeros_like(buf[0:k])

        @pl.when(row == GRID_R - 1)
        def _():
            buf[TH + k :] = jnp.zeros_like(buf[TH + k :])

        @pl.when(col == 0)
        def _():
            buf[:, 0:k] = jnp.zeros_like(buf[:, 0:k])

        @pl.when(col == GRID_C - 1)
        def _():
            buf[:, TW + k :] = jnp.zeros_like(buf[:, TW + k :])

    halos = ((hact, 1, 0), (h0, 2, 1), (hsec, 1, 2), (h2, 2, 3), (hs, 3, 4), (hg, 4, 5))
    for buf, k, _ in halos:
        clear_outside(buf, k)

    barrier = pltpu.get_barrier_semaphore()

    def greet(device):
        pl.semaphore_signal(barrier, inc=1, device_id=device, device_id_type=MESH)

    block = lax.div(wa, 2)
    same = block == col

    @pl.loop(0, 8)
    def _(step):
        r = ha * 8 + lax.rem(spot + step, 8)

        @pl.when(jnp.logical_not((step == 0) & same))
        def _():
            greet(owner(r, block))

        a, b = lax.div(step, 2), 2 * col + lax.rem(step, 2)

        @pl.when(jnp.logical_not((a == ta) & (b == wa)))
        def _():
            greet(at(a, ha, b))

    planes = [z * 4, lax.rem(z + 1, 8) * 4]
    for a in range(4):
        for b in range(4):
            itself = first & (a == ta) & (b == low)

            @pl.when(jnp.logical_not(itself))
            def _():
                greet(at(a, ha, planes[b // 2] + b))
                greet(at(a, ha, spot * 4 + b))

    near_count = 0
    for dr, dc in SIDES:
        near_count = near_count + there(dr, dc).astype(jnp.int32)

        @pl.when(there(dr, dc))
        def _():
            greet(near(dr, dc))

    pl.semaphore_wait(
        barrier, 48 - 2 * same.astype(jnp.int32) - 2 * first.astype(jnp.int32) + near_count
    )

    for step in FAR_FIRST:
        to = lax.rem(spot + step, 8)
        source = tin.at[:, pl.ds(to * TH, TH)]
        target = xin.at[pl.ds(ta * 2, 2), :, lax.rem(wa, 2)]

        def send_patch():
            pltpu.make_async_remote_copy(
                src_ref=source,
                dst_ref=target,
                send_sem=xsend,
                recv_sem=xrecv,
                device_id=owner(ha * 8 + to, block),
                device_id_type=MESH,
            ).start()

        if step:
            send_patch()
        else:
            @pl.when(same)
            def _():
                pltpu.make_async_copy(source, target, xrecv).start()

            pl.when(jnp.logical_not(same))(send_patch)

    @pl.loop(0, 16)
    def _(step):
        c = lax.rem(col + step, 16)
        source, target = sin.at[:, pl.ds(c * 2, 2)], rin.at[pl.ds(ta * 2, 2), low]
        itself = first & (step == 0)

        @pl.when(itself)
        def _():
            pltpu.make_async_copy(source, target, rrecv).start()

        @pl.when(jnp.logical_not(itself))
        def _():
            pltpu.make_async_remote_copy(
                src_ref=source,
                dst_ref=target,
                send_sem=rsend,
                recv_sem=rrecv,
                device_id=owner(held, c),
                device_id_type=MESH,
            ).start()

    for copy in small + weights:
        copy.start()
    af[:, :, :, CS:WIDE] = jnp.zeros((TH + 2, TW + 2, 8, WIDE - CS), F32)
    wb[:, :, :, :, CT:WIDE, :] = jnp.zeros((2, 3, 3, 3, WIDE - CT, CT), BF16)

    def side_copy(buf, k, slot, d):
        dr, dc = SIDES[d]

        def source(side, size):
            return pl.ds(*{-1: (k, k), 0: (k, size), 1: (size, k)}[side])

        def target(side, size):
            return pl.ds(*{-1: (size + k, k), 0: (k, size), 1: (0, k)}[side])

        return pltpu.make_async_remote_copy(
            src_ref=buf.at[source(dr, TH), source(dc, TW)],
            dst_ref=buf.at[target(dr, TH), target(dc, TW)],
            send_sem=hsend.at[slot, d],
            recv_sem=hrecv.at[slot, d],
            device_id=near(dr, dc),
            device_id_type=MESH,
        )

    def send(buf, k, slot):
        for d, (dr, dc) in enumerate(SIDES):
            @pl.when(there(dr, dc))
            def _():
                side_copy(buf, k, slot, d).start()

    def receive(buf, k, slot):
        for d, (dr, dc) in enumerate(SIDES):
            @pl.when(there(-dr, -dc))
            def _():
                side_copy(buf, k, slot, d).wait_recv()

    def drain(buf, k, slot):
        for d, (dr, dc) in enumerate(SIDES):
            @pl.when(there(dr, dc))
            def _():
                side_copy(buf, k, slot, d).wait_send()

    def ring(k):
        rows, cols = TH + 2 * k, TW + 2 * k
        return [
            (slice(0, k), slice(0, cols)),
            (slice(TH + k, rows), slice(0, cols)),
            (slice(k, TH + k), slice(0, k)),
            (slice(k, TH + k), slice(TW + k, cols)),
        ]

    frames = lax.broadcasted_iota(jnp.int32, (1, 8, CS), 1)
    wide_frames = lax.broadcasted_iota(jnp.int32, (1, 8, CT), 1)

    def taps(src, h, start, width, n):
        acc = [None] * 3
        for j in range(3):
            for l in range(3):
                x = src[h + j, start + l : start + l + width]
                for i in range(3):
                    term = x * dwv[i, j, l, n : n + 1, :].reshape(1, 1, CS)
                    acc[i] = term if acc[i] is None else acc[i] + term
        return acc[2] + shifted(acc[1], 1, frames) + shifted(acc[0], 2, frames)

    def taps_back(h, start, pairs, n):
        acc = [None] * 3
        for j in range(3):
            for l in range(3):
                held_at = pb if l == 1 else pa
                first_pair = start + l // 2
                x = held_at[h + j, first_pair : first_pair + pairs]
                for i in range(3):
                    term = x * kb[n, i, 2 - j, 2 - l]
                    acc[i] = term if acc[i] is None else acc[i] + term
        acc = [a.astype(F32).reshape(2 * pairs, 8, CS) for a in acc]
        return acc[2] + shifted(acc[1], -1, frames) + shifted(acc[0], -2, frames)

    def conv(b):
        for j in range(3):
            for l in range(3):
                at_lane = (j * 3 + l) * WIDE
                lhs[:, at_lane : at_lane + WIDE] = (
                    af[j : j + TH, l : l + TW].reshape(512, WIDE).astype(BF16)
                )
        for i in range(3):
            weights[b * 3 + i].wait()
            pp[i] = jnp.dot(
                lhs[...], wb[b, i].reshape(9 * WIDE, CT), preferred_element_type=F32
            )

    def conv_row(m):
        p = [pp[i, pl.ds(m * 64, 64)].reshape(8, 8, CT) for i in range(3)]
        return p[2] + shifted(p[1], 1, wide_frames) + shifted(p[0], 2, wide_frames)

    for copy in small:
        copy.wait()
    for n in range(4):
        for i in range(3):
            for j in range(3):
                for l in range(3):
                    kb[n, i, j, l] = jnp.broadcast_to(
                        dwv[i, j, l, n : n + 1, :], (16, CS)
                    ).astype(BF16)

    pltpu.make_async_copy(rin, rin, rrecv).wait()
    rf[...] = rin[...].astype(F32).reshape(512, CS)

    @pl.loop(0, TH)
    def _(h):
        for w in range(TW):
            s = rf[pl.ds(h * TW + w, 8, stride=64), :]
            s0f[h + 2, w + 2] = s
            h0[h + 2, w + 2] = s.astype(BF16)
            u, slope = act(s)
            u20[h + 2, w + 2] = u
            sl0[h, w] = slope

    send(h0, 2, 1)

    pltpu.make_async_copy(xin, xin, xrecv).wait()
    xall = xin[...].astype(F32).reshape(512, CT)
    xf[0] = xall[:, 0:CS]
    xf[1, :, 0 : CT - CS] = xall[:, CS:CT]

    @pl.loop(0, TH)
    def _(h):
        for w in range(TW):
            spot = pl.ds(h * TW + w, 8, stride=64)
            x = jnp.concatenate([xf[0, spot, :], xf[1, spot, :][:, 0 : CT - CS]], axis=-1)
            xt[h, w] = x
            a = silu_norm(x)
            hact[h + 1, w + 1] = a.astype(BF16)
            af[h + 1, w + 1, :, 0:CT] = a

    send(hact, 1, 0)

    def wide_layer(n, field):
        @pl.loop(0, TH + 2)
        def _(h):
            for w in (0, 9):
                d18[h, w : w + 9] = taps(u20, h, w, 9, n)

        mm18[...] = jnp.dot(
            d18[...].reshape(864, CS).astype(BF16), pwv[n], preferred_element_type=F32
        ).reshape(6, 18, 8, CS)

        @pl.loop(0, TH + 2)
        def _(h):
            s = field[h + 1, 1:19] + mm18[h]
            mm18[h] = s
            u, slope = act(s)
            u18[h] = u
            sl1[h] = slope

        clear_outside(u18, 1)

    def narrow_layer(n):
        @pl.loop(0, TH)
        def _(h):
            for w in (0, 8):
                d16[h, w : w + 8] = taps(u18, h, w, 8, n)

        mm16[...] = jnp.dot(
            d16[...].reshape(512, CS).astype(BF16), pwv[n], preferred_element_type=F32
        ).reshape(4, 16, 8, CS)

    receive(h0, 2, 1)
    for rows, cols in ring(2):
        s = h0[rows, cols].astype(F32)
        s0f[rows, cols] = s
        u20[rows, cols] = act(s)[0]
    wide_layer(0, s0f)
    narrow_layer(1)

    @pl.loop(0, TH)
    def _(h):
        s = mm18[h + 1, 1:17] + mm16[h]
        s2f[h + 2, 2:18] = s
        h2[h + 2, 2:18] = s.astype(BF16)
        u, slope = act(s)
        u20[h + 2, 2:18] = u
        sl2[h + 2, 2:18] = slope

    send(h2, 2, 3)

    receive(hact, 1, 0)
    for rows, cols in ring(1):
        af[rows, cols, :, 0:CT] = hact[rows, cols].astype(F32)
    conv(0)

    @pl.loop(0, 8)
    def _(m):
        h, w = lax.div(m, 2), lax.rem(m, 2) * 8
        a = silu_norm(conv_row(m))
        hsec[h + 1, pl.ds(w + 1, 8)] = a.astype(BF16)
        af[h + 1, pl.ds(w + 1, 8), :, 0:CT] = a

    send(hsec, 1, 2)

    receive(h2, 2, 3)
    for rows, cols in ring(2):
        s = h2[rows, cols].astype(F32)
        s2f[rows, cols] = s
        u, slope = act(s)
        u20[rows, cols] = u
        sl2[rows, cols] = slope

    @pl.loop(0, TH + 2)
    def _(h):
        for w in (0, 9):
            d18[h, w : w + 9] = taps(u20, h, w, 9, 2)

    mm18[...] = jnp.dot(
        d18[...].reshape(864, CS).astype(BF16), pwv[2], preferred_element_type=F32
    ).reshape(6, 18, 8, CS)

    @pl.loop(0, TH + 2)
    def _(h):
        s = s2f[h + 1, 1:19] + mm18[h]
        mm18[h] = s
        u, slope = act(s)
        u18[h] = u
        d18[h] = slope

    hs[3:7, 3:19] = d18[1:5, 1:17].astype(BF16)
    send(hs, 3, 4)
    clear_outside(u18, 1)
    narrow_layer(3)
    s4b[...] = (mm18[1:5, 1:17] + mm16[...]).reshape(512, CS).astype(BF16)

    pr[...] = lax.dot_general(s4b[...], projv[...], TRANSPOSED, preferred_element_type=F32)

    receive(hsec, 1, 2)
    for rows, cols in ring(1):
        af[rows, cols, :, 0:CT] = hsec[rows, cols].astype(F32)
    conv(1)

    @pl.loop(0, 8)
    def _(m):
        h, w = lax.div(m, 2), lax.rem(m, 2) * 8
        target = (xt[h, pl.ds(w, 8)] + conv_row(m)).reshape(64, CT)
        span = pl.ds(m * 64, 64)
        mb[span] = (pr[span] - target).astype(BF16)

    g = jnp.dot(mb[...], projv[...], preferred_element_type=F32).reshape(4, 16, 8, CS)
    gf[4:8, 4:20] = g
    hg[4:8, 4:20] = g.astype(BF16)
    send(hg, 4, 5)

    receive(hs, 3, 4)
    receive(hg, 4, 5)
    for rows, cols in ring(4):
        gf[rows, cols] = hg[rows, cols].astype(F32)

    def back(n, source, k):
        rows, cols = TH + 2 * k, TW + 2 * k
        eb[0:rows, 0:cols] = lax.dot_general(
            source[...].reshape(rows * cols * 8, CS).astype(BF16),
            pwv[n],
            TRANSPOSED,
            preferred_element_type=F32,
        ).reshape(rows, cols, 8, CS)
        half = cols // 2

        @pl.loop(0, rows)
        def _(h):
            pa[h, 0:half] = eb[h, 0:cols].reshape(half, 16, CS).astype(BF16)
            pb[h, 0 : half - 1] = eb[h, 1 : cols - 1].reshape(half - 1, 16, CS).astype(BF16)

    back(3, gf, 4)

    @pl.loop(0, 10)
    def _(h):
        slope = hs[h].astype(F32)
        g22[h] = gf[h + 1, 1:23] + taps_back(h, 0, 11, 3) * slope

    clear_outside(g22, 3)
    back(2, g22, 3)

    @pl.loop(0, 8)
    def _(h):
        g20[h] = g22[h + 1, 1:21] + taps_back(h, 0, 10, 2) * sl2[h]

    clear_outside(g20, 2)
    back(1, g20, 2)

    @pl.loop(0, 6)
    def _(h):
        d18[h] = g20[h + 1, 1:19] + taps_back(h, 0, 9, 1) * sl1[h]

    clear_outside(d18, 1)
    back(0, d18, 1)

    def send_back(x, h):
        pltpu.make_async_remote_copy(
            src_ref=ob.at[pl.ds(x * 2, 2), h],
            dst_ref=out.at[:, pl.ds(col * 2, 2)],
            send_sem=osend,
            recv_sem=orecv,
            device_id=at(x, ha, spot * 4 + h),
            device_id_type=MESH,
        ).start()

    @pl.loop(0, TH)
    def _(h):
        g = d18[h + 1, 1:17] + taps_back(h, 0, 8, 0) * sl0[h]
        rf[pl.ds(h * 128, 128)] = g.reshape(128, CS)
        for half in range(2):
            for t in range(8):
                ob[t, h, half] = rf[
                    pl.ds(h * 128 + half * 64 + t, 8, stride=8), :
                ].astype(BF16)
        for step in (2, 1, 3):
            send_back(lax.rem(ta + step, 4), h)

        @pl.when(first & (h == low))
        def _():
            pltpu.make_async_copy(
                ob.at[pl.ds(ta * 2, 2), h], out.at[:, pl.ds(col * 2, 2)], orecv
            ).start()

        @pl.when(jnp.logical_not(first & (h == low)))
        def _():
            send_back(ta, h)

    for buf, k, slot in halos:
        drain(buf, k, slot)

    @pl.when(same)
    def _():
        part = tin.at[:, 0:28]
        pltpu.make_async_copy(part, part, xsend).wait()

    @pl.when(jnp.logical_not(same))
    def _():
        pltpu.make_async_copy(tin, tin, xsend).wait()

    for sem in (rsend, osend):
        @pl.when(first)
        def _():
            part = sin.at[:, 0:30]
            pltpu.make_async_copy(part, part, sem).wait()

        @pl.when(jnp.logical_not(first))
        def _():
            pltpu.make_async_copy(sin, sin, sem).wait()

    pltpu.make_async_copy(out, out, orecv).wait()


def on_device(tin, tw, sin, dw, pw, proj):
    anywhere = pl.BlockSpec(memory_space=pl.ANY)
    dma = pltpu.SemaphoreType.DMA

    def tile(k, c, kind):
        return pltpu.VMEM((TH + 2 * k, TW + 2 * k, 8, c), kind)

    scratch = [
        pltpu.VMEM((8, TH, 2, 8, CT), BF16),
        pltpu.VMEM((2, 512, CS), F32),
        tile(0, CT, F32),
        tile(1, CT, BF16),
        tile(1, CT, BF16),
        tile(1, WIDE, F32),
        pltpu.VMEM((512, 9 * WIDE), BF16),
        pltpu.VMEM((2, 3, 3, 3, WIDE, CT), BF16),
        pltpu.VMEM((3, 512, CT), F32),
        pltpu.VMEM((8, TH, 2, 8, CS), BF16),
        pltpu.VMEM((512, CS), F32),
        tile(2, CS, F32),
        tile(2, CS, F32),
        tile(2, CS, F32),
        tile(1, CS, F32),
        tile(1, CS, F32),
        tile(1, CS, F32),
        tile(0, CS, F32),
        tile(0, CS, F32),
        tile(0, CS, F32),
        tile(1, CS, F32),
        tile(2, CS, F32),
        tile(2, CS, BF16),
        tile(2, CS, BF16),
        tile(3, CS, BF16),
        tile(4, CS, BF16),
        tile(4, CS, F32),
        tile(4, CS, F32),
        pltpu.VMEM((12, 12, 16, CS), BF16),
        pltpu.VMEM((12, 11, 16, CS), BF16),
        pltpu.VMEM((4, 3, 3, 3, 16, CS), BF16),
        tile(3, CS, F32),
        tile(2, CS, F32),
        pltpu.VMEM((512, CS), BF16),
        pltpu.VMEM((512, CT), BF16),
        pltpu.VMEM((512, CT), F32),
        pltpu.VMEM((8, TH, 2, 8, CS), BF16),
        pltpu.VMEM((3, 3, 3, 4, CS), F32),
        pltpu.VMEM((4, CS, CS), BF16),
        pltpu.VMEM((CT, CS), BF16),
        dma((9,)),
        dma(()),
        dma(()),
        dma(()),
        dma(()),
        dma(()),
        dma(()),
        dma((6, 8)),
        dma((6, 8)),
    ]
    result = pl.pallas_call(
        kernel,
        out_shape=jax.ShapeDtypeStruct((2, 32, 8, CS), BF16),
        in_specs=[anywhere] * 6,
        out_specs=anywhere,
        scratch_shapes=scratch,
        compiler_params=pltpu.CompilerParams(
            collective_id=0, has_side_effects=True, vmem_limit_bytes=56 * 1024 * 1024
        ),
    )(tin, tw, sin.reshape(2, 32, 8, CS), dw.transpose(1, 2, 3, 0, 4), pw, proj.T)
    return result.reshape(2, 1, 256, CS)


def solution(mesh):
    rows = P("ta", ("ha", "wa"), None, None)
    return jax.shard_map(
        on_device,
        mesh=mesh,
        in_specs=(P("ta", "ha", "wa", None), P(), rows, P(), P(), P()),
        out_specs=rows,
        check_vma=False,
    )
```

```python
import jax
import jax.numpy as jnp
from jax import lax
from jax.experimental import pallas as pl
from jax.experimental.pallas import tpu as pltpu
from jax.sharding import PartitionSpec as P

MESH = pl.DeviceIdType.MESH
F32, BF16 = jnp.float32, jnp.bfloat16
SIDES = [(-1, 0), (1, 0), (-1, -1), (-1, 1), (1, -1), (1, 1), (0, -1), (0, 1)]
FAR_FIRST = (4, 3, 5, 2, 6, 1, 7, 0)
CT, CS, WIDE = 192, 128, 256
TH, TW = 4, 16
GRID_R, GRID_C = 32, 16
TRANSPOSED = (((1,), (1,)), ((), ()))


def rational(x):
    gate = 0.5 * jnp.tanh(0.5 * x) + 0.5
    return x * gate


def act(s):
    gate = 0.5 * jnp.tanh(0.5 * s) + 0.5
    u = s * gate
    return u, gate + u * (1.0 - gate)


def silu_norm(x):
    scale = lax.rsqrt(jnp.sum(x * x, axis=-1, keepdims=True) * (1.0 / CT) + 1e-06)
    return rational(x * scale)


def shifted(v, by, frames):
    if by > 0:
        return jnp.where(frames >= by, pltpu.roll(v, by, v.ndim - 2), 0.0)
    return jnp.where(frames < 8 + by, pltpu.roll(v, 8 + by, v.ndim - 2), 0.0)


def kernel(
    tin, tw, sin, dw, pw, proj, out,
    xin, xf, xt, hact, hsec, af, lhs, wb, pp,
    rin, rf, s0f, s2f, u20, u18, d18, mm18, d16, mm16, sl0, sl1, sl2,
    h0, h2, hs, hg, gf, eb, g22, g20, s4b, mb, pr, ob, dwv, pwv, projv,
    wsem, xsend, xrecv, rsend, rrecv, osend, orecv, hsend, hrecv,
):
    ta, ha, wa = lax.axis_index("ta"), lax.axis_index("ha"), lax.axis_index("wa")
    z, low = lax.div(wa, 4), lax.rem(wa, 4)

    def bent(p):
        return jnp.where(p < 2, p, 5 - p)

    def place(a, b):
        p = bent(b)
        return a * 4 + jnp.where(lax.rem(a, 2) == 0, p, 3 - p)

    upper = lax.div(low, 2)
    spot, col = lax.rem(z + 8 - upper, 8), place(ta, low)
    row, held = ha * 8 + spot, ha * 8 + z
    first = upper == 0

    def at(a, b, c):
        return {"ta": a, "ha": b, "wa": c}

    def owner(r, c):
        a, p = lax.div(c, 4), lax.rem(c, 4)
        p = bent(jnp.where(lax.rem(a, 2) == 0, p, 3 - p))
        return at(a, lax.div(r, 8), lax.rem(lax.rem(r, 8) + lax.div(p, 2), 8) * 4 + p)

    neighbours = {side: owner(row + side[0], col + side[1]) for side in SIDES}
    fits_row = {-1: row > 0, 0: row >= 0, 1: row < GRID_R - 1}
    fits_col = {-1: col > 0, 0: col >= 0, 1: col < GRID_C - 1}
    present = {side: fits_row[side[0]] & fits_col[side[1]] for side in SIDES}

    def near(dr, dc):
        return neighbours[dr, dc]

    def there(dr, dc):
        return present[dr, dc]

    weights = []
    for b in range(2):
        for i in range(3):
            weights.append(
                pltpu.make_async_copy(
                    tw.at[0, b, i], wb.at[b, i, :, :, 0:CT, :], wsem.at[b * 3 + i]
                )
            )
    small = [
        pltpu.make_async_copy(dw, dwv, wsem.at[6]),
        pltpu.make_async_copy(pw, pwv, wsem.at[7]),
        pltpu.make_async_copy(proj, projv, wsem.at[8]),
    ]
    def clear_outside(buf, k):
        @pl.when(row == 0)
        def _():
            buf[0:k] = jnp.zeros_like(buf[0:k])

        @pl.when(row == GRID_R - 1)
        def _():
            buf[TH + k :] = jnp.zeros_like(buf[TH + k :])

        @pl.when(col == 0)
        def _():
            buf[:, 0:k] = jnp.zeros_like(buf[:, 0:k])

        @pl.when(col == GRID_C - 1)
        def _():
            buf[:, TW + k :] = jnp.zeros_like(buf[:, TW + k :])

    halos = ((hact, 1, 0), (h0, 2, 1), (hsec, 1, 2), (h2, 2, 3), (hs, 3, 4), (hg, 4, 5), (hg, 4, 6))
    for buf, k, _ in halos[:6]:
        clear_outside(buf, k)

    barrier = pltpu.get_barrier_semaphore()

    def greet(device):
        pl.semaphore_signal(barrier, inc=1, device_id=device, device_id_type=MESH)

    block = lax.div(wa, 2)
    same = block == col

    @pl.loop(0, 8)
    def _(step):
        r = ha * 8 + lax.rem(spot + step, 8)

        @pl.when(jnp.logical_not((step == 0) & same))
        def _():
            greet(owner(r, block))

        a, b = lax.div(step, 2), 2 * col + lax.rem(step, 2)

        @pl.when(jnp.logical_not((a == ta) & (b == wa)))
        def _():
            greet(at(a, ha, b))

    planes = [z * 4, lax.rem(z + 1, 8) * 4]
    for a in range(4):
        for b in range(4):
            itself = first & (a == ta) & (b == low)

            @pl.when(jnp.logical_not(itself))
            def _():
                greet(at(a, ha, planes[b // 2] + b))
                greet(at(a, ha, spot * 4 + b))

    near_count = 0
    for dr, dc in SIDES:
        near_count = near_count + there(dr, dc).astype(jnp.int32)

        @pl.when(there(dr, dc))
        def _():
            greet(near(dr, dc))

    pl.semaphore_wait(
        barrier, 48 - 2 * same.astype(jnp.int32) - 2 * first.astype(jnp.int32) + near_count
    )

    for step in FAR_FIRST:
        to = lax.rem(spot + step, 8)
        source = tin.at[:, pl.ds(to * TH, TH)]
        target = xin.at[pl.ds(ta * 2, 2), :, lax.rem(wa, 2)]

        def send_patch():
            pltpu.make_async_remote_copy(
                src_ref=source,
                dst_ref=target,
                send_sem=xsend,
                recv_sem=xrecv,
                device_id=owner(ha * 8 + to, block),
                device_id_type=MESH,
            ).start()

        if step:
            send_patch()
        else:
            @pl.when(same)
            def _():
                pltpu.make_async_copy(source, target, xrecv).start()

            pl.when(jnp.logical_not(same))(send_patch)

    @pl.loop(0, 16)
    def _(step):
        c = lax.rem(col + step, 16)
        source, target = sin.at[:, pl.ds(c * 2, 2)], rin.at[pl.ds(ta * 2, 2), low]
        itself = first & (step == 0)

        @pl.when(itself)
        def _():
            pltpu.make_async_copy(source, target, rrecv).start()

        @pl.when(jnp.logical_not(itself))
        def _():
            pltpu.make_async_remote_copy(
                src_ref=source,
                dst_ref=target,
                send_sem=rsend,
                recv_sem=rrecv,
                device_id=owner(held, c),
                device_id_type=MESH,
            ).start()

    for copy in small + weights:
        copy.start()
    af[:, :, :, CS:WIDE] = jnp.zeros((TH + 2, TW + 2, 8, WIDE - CS), F32)
    wb[:, :, :, :, CT:WIDE, :] = jnp.zeros((2, 3, 3, 3, WIDE - CT, CT), BF16)

    def side_copy(buf, k, slot, d):
        dr, dc = SIDES[d]
        cut = slice(None)
        if slot > 4:
            cut = pl.ds((slot - 5) * 2, 2)

        def source(side, size):
            return pl.ds(*{-1: (k, k), 0: (k, size), 1: (size, k)}[side])

        def target(side, size):
            return pl.ds(*{-1: (size + k, k), 0: (k, size), 1: (0, k)}[side])

        return pltpu.make_async_remote_copy(
            src_ref=buf.at[source(dr, TH), source(dc, TW)].at[cut],
            dst_ref=buf.at[target(dr, TH), target(dc, TW)].at[cut],
            send_sem=hsend.at[slot, d],
            recv_sem=hrecv.at[slot, d],
            device_id=near(dr, dc),
            device_id_type=MESH,
        )

    def send(buf, k, slot):
        for d, (dr, dc) in enumerate(SIDES):
            @pl.when(there(dr, dc))
            def _():
                side_copy(buf, k, slot, d).start()

    def receive(buf, k, slot):
        for d, (dr, dc) in enumerate(SIDES):
            @pl.when(there(-dr, -dc))
            def _():
                side_copy(buf, k, slot, d).wait_recv()

    def drain(buf, k, slot):
        for d, (dr, dc) in enumerate(SIDES):
            @pl.when(there(dr, dc))
            def _():
                side_copy(buf, k, slot, d).wait_send()

    def ring(k):
        rows, cols = TH + 2 * k, TW + 2 * k
        return [
            (slice(0, k), slice(0, cols)),
            (slice(TH + k, rows), slice(0, cols)),
            (slice(k, TH + k), slice(0, k)),
            (slice(k, TH + k), slice(TW + k, cols)),
        ]

    frames = lax.broadcasted_iota(jnp.int32, (1, 8, CS), 1)
    wide_frames = lax.broadcasted_iota(jnp.int32, (1, 8, CT), 1)

    def taps(src, h, start, width, n, flip):
        acc = [None] * 3
        for j in range(3):
            for l in range(3):
                x = src[h + j, start + l : start + l + width]
                for i in range(3):
                    jj, ll = (2 - j, 2 - l) if flip else (j, l)
                    term = x * dwv[i, jj, ll, n : n + 1, :].reshape(1, 1, CS)
                    acc[i] = term if acc[i] is None else acc[i] + term
        sign = -1 if flip else 1
        return acc[2] + shifted(acc[1], sign, frames) + shifted(acc[0], 2 * sign, frames)

    def gather_taps():
        for j in range(3):
            for l in range(3):
                at_lane = (j * 3 + l) * WIDE
                lhs[:, at_lane : at_lane + WIDE] = (
                    af[j : j + TH, l : l + TW].reshape(512, WIDE).astype(BF16)
                )

    def conv(b, begin, rows):
        for i in range(3):
            pp[i, begin : begin + rows] = jnp.dot(
                lhs[begin : begin + rows],
                wb[b, i].reshape(9 * WIDE, CT),
                preferred_element_type=F32,
            )

    def conv_row(m):
        p = [pp[i, pl.ds(m * 64, 64)].reshape(8, 8, CT) for i in range(3)]
        return p[2] + shifted(p[1], 1, wide_frames) + shifted(p[0], 2, wide_frames)

    pltpu.make_async_copy(rin, rin, rrecv).wait()
    rf[...] = rin[...].astype(F32).reshape(512, CS)

    @pl.loop(0, TH)
    def _(h):
        for w in range(TW):
            s = rf[pl.ds(h * TW + w, 8, stride=64), :]
            s0f[h + 2, w + 2] = s
            h0[h + 2, w + 2] = s.astype(BF16)
            u, slope = act(s)
            u20[h + 2, w + 2] = u
            sl0[h, w] = slope

    send(h0, 2, 1)

    pltpu.make_async_copy(xin, xin, xrecv).wait()
    xall = xin[...].astype(F32).reshape(512, CT)
    xf[0] = xall[:, 0:CS]
    xf[1, :, 0 : CT - CS] = xall[:, CS:CT]

    @pl.loop(0, TH)
    def _(h):
        for w in range(TW):
            spot = pl.ds(h * TW + w, 8, stride=64)
            x = jnp.concatenate([xf[0, spot, :], xf[1, spot, :][:, 0 : CT - CS]], axis=-1)
            xt[h, w] = x
            a = silu_norm(x)
            hact[h + 1, w + 1] = a.astype(BF16)
            af[h + 1, w + 1, :, 0:CT] = a

    send(hact, 1, 0)

    for copy in small:
        copy.wait()

    def wide_layer(n, field):
        @pl.loop(0, TH + 2)
        def _(h):
            for w in (0, 9):
                d18[h, w : w + 9] = taps(u20, h, w, 9, n, False)

        mm18[...] = jnp.dot(
            d18[...].reshape(864, CS).astype(BF16), pwv[n], preferred_element_type=F32
        ).reshape(6, 18, 8, CS)

        @pl.loop(0, TH + 2)
        def _(h):
            s = field[h + 1, 1:19] + mm18[h]
            mm18[h] = s
            u, slope = act(s)
            u18[h] = u
            sl1[h] = slope

        clear_outside(u18, 1)

    def narrow_layer(n):
        @pl.loop(0, TH)
        def _(h):
            for w in (0, 8):
                d16[h, w : w + 8] = taps(u18, h, w, 8, n, False)

        mm16[...] = jnp.dot(
            d16[...].reshape(512, CS).astype(BF16), pwv[n], preferred_element_type=F32
        ).reshape(4, 16, 8, CS)

    receive(h0, 2, 1)
    for rows, cols in ring(2):
        s = h0[rows, cols].astype(F32)
        s0f[rows, cols] = s
        u20[rows, cols] = act(s)[0]
    wide_layer(0, s0f)
    narrow_layer(1)

    @pl.loop(0, TH)
    def _(h):
        s = mm18[h + 1, 1:17] + mm16[h]
        s2f[h + 2, 2:18] = s
        h2[h + 2, 2:18] = s.astype(BF16)
        u, slope = act(s)
        u20[h + 2, 2:18] = u
        sl2[h + 2, 2:18] = slope

    send(h2, 2, 3)

    receive(hact, 1, 0)
    for rows, cols in ring(1):
        af[rows, cols, :, 0:CT] = hact[rows, cols].astype(F32)
    gather_taps()
    for copy in weights[:3]:
        copy.wait()
    conv(0, 0, 512)

    @pl.loop(0, 8)
    def _(m):
        h, w = lax.div(m, 2), lax.rem(m, 2) * 8
        a = silu_norm(conv_row(m))
        hsec[h + 1, pl.ds(w + 1, 8)] = a.astype(BF16)
        af[h + 1, pl.ds(w + 1, 8), :, 0:CT] = a

    send(hsec, 1, 2)

    receive(h2, 2, 3)
    for rows, cols in ring(2):
        s = h2[rows, cols].astype(F32)
        s2f[rows, cols] = s
        u, slope = act(s)
        u20[rows, cols] = u
        sl2[rows, cols] = slope

    @pl.loop(0, TH + 2)
    def _(h):
        for w in (0, 9):
            d18[h, w : w + 9] = taps(u20, h, w, 9, 2, False)

    mm18[...] = jnp.dot(
        d18[...].reshape(864, CS).astype(BF16), pwv[2], preferred_element_type=F32
    ).reshape(6, 18, 8, CS)

    @pl.loop(0, TH + 2)
    def _(h):
        s = s2f[h + 1, 1:19] + mm18[h]
        mm18[h] = s
        u, slope = act(s)
        u18[h] = u
        d18[h] = slope

    hs[3:7, 3:19] = d18[1:5, 1:17].astype(BF16)
    send(hs, 3, 4)
    clear_outside(u18, 1)
    narrow_layer(3)
    s4b[...] = (mm18[1:5, 1:17] + mm16[...]).reshape(512, CS).astype(BF16)

    pr[...] = lax.dot_general(s4b[...], projv[...], TRANSPOSED, preferred_element_type=F32)

    receive(hsec, 1, 2)
    for rows, cols in ring(1):
        af[rows, cols, :, 0:CT] = hsec[rows, cols].astype(F32)
    gather_taps()
    for copy in weights[3:]:
        copy.wait()
    for half in range(2):
        conv(1, half * 256, 256)

        @pl.loop(half * 4, half * 4 + 4)
        def _(m):
            h, w = lax.div(m, 2), lax.rem(m, 2) * 8
            target = (xt[h, pl.ds(w, 8)] + conv_row(m)).reshape(64, CT)
            span = pl.ds(m * 64, 64)
            mb[span] = (pr[span] - target).astype(BF16)

        g = jnp.dot(
            mb[half * 256 : half * 256 + 256], projv[...], preferred_element_type=F32
        ).reshape(2, 16, 8, CS)
        gf[half * 2 + 4 : half * 2 + 6, 4:20] = g
        hg[half * 2 + 4 : half * 2 + 6, 4:20] = g.astype(BF16)
        send(hg, 4, 5 + half)

    receive(hs, 3, 4)
    receive(hg, 4, 5)
    receive(hg, 4, 6)
    for rows, cols in ring(4):
        gf[rows, cols] = hg[rows, cols].astype(F32)

    def back(n, source, k):
        rows, cols = TH + 2 * k, TW + 2 * k
        eb[0:rows, 0:cols] = lax.dot_general(
            source[...].reshape(rows * cols * 8, CS).astype(BF16),
            pwv[n],
            TRANSPOSED,
            preferred_element_type=F32,
        ).reshape(rows, cols, 8, CS)

    back(3, gf, 4)

    @pl.loop(0, 10)
    def _(h):
        for w in (0, 11):
            slope = hs[h, w : w + 11].astype(F32)
            g22[h, w : w + 11] = (
                gf[h + 1, w + 1 : w + 12] + taps(eb, h, w, 11, 3, True) * slope
            )

    clear_outside(g22, 3)
    back(2, g22, 3)

    @pl.loop(0, 8)
    def _(h):
        for w in (0, 10):
            g20[h, w : w + 10] = (
                g22[h + 1, w + 1 : w + 11]
                + taps(eb, h, w, 10, 2, True) * sl2[h, w : w + 10]
            )

    clear_outside(g20, 2)
    back(1, g20, 2)

    @pl.loop(0, 6)
    def _(h):
        for w in (0, 9):
            d18[h, w : w + 9] = (
                g20[h + 1, w + 1 : w + 10]
                + taps(eb, h, w, 9, 1, True) * sl1[h, w : w + 9]
            )

    clear_outside(d18, 1)
    back(0, d18, 1)

    def send_back(x, h):
        pltpu.make_async_remote_copy(
            src_ref=ob.at[pl.ds(x * 2, 2), h],
            dst_ref=out.at[:, pl.ds(col * 2, 2)],
            send_sem=osend,
            recv_sem=orecv,
            device_id=at(x, ha, spot * 4 + h),
            device_id_type=MESH,
        ).start()

    @pl.loop(0, TH)
    def _(h):
        for w in (0, 8):
            g = (
                d18[h + 1, w + 1 : w + 9]
                + taps(eb, h, w, 8, 0, True) * sl0[h, w : w + 8]
            )
            rf[pl.ds(h * 128 + w * 8, 64)] = g.reshape(64, CS)
        for half in range(2):
            for t in range(8):
                ob[t, h, half] = rf[
                    pl.ds(h * 128 + half * 64 + t, 8, stride=8), :
                ].astype(BF16)
        for step in (2, 1, 3):
            send_back(lax.rem(ta + step, 4), h)

        @pl.when(first & (h == low))
        def _():
            pltpu.make_async_copy(
                ob.at[pl.ds(ta * 2, 2), h], out.at[:, pl.ds(col * 2, 2)], orecv
            ).start()

        @pl.when(jnp.logical_not(first & (h == low)))
        def _():
            send_back(ta, h)

    for buf, k, slot in halos:
        drain(buf, k, slot)

    @pl.when(same)
    def _():
        part = tin.at[:, 0:28]
        pltpu.make_async_copy(part, part, xsend).wait()

    @pl.when(jnp.logical_not(same))
    def _():
        pltpu.make_async_copy(tin, tin, xsend).wait()

    for sem in (rsend, osend):
        @pl.when(first)
        def _():
            part = sin.at[:, 0:30]
            pltpu.make_async_copy(part, part, sem).wait()

        @pl.when(jnp.logical_not(first))
        def _():
            pltpu.make_async_copy(sin, sin, sem).wait()

    pltpu.make_async_copy(out, out, orecv).wait()


def on_device(tin, tw, sin, dw, pw, proj):
    anywhere = pl.BlockSpec(memory_space=pl.ANY)
    dma = pltpu.SemaphoreType.DMA

    def tile(k, c, kind):
        return pltpu.VMEM((TH + 2 * k, TW + 2 * k, 8, c), kind)

    scratch = [
        pltpu.VMEM((8, TH, 2, 8, CT), BF16),
        pltpu.VMEM((2, 512, CS), F32),
        tile(0, CT, F32),
        tile(1, CT, BF16),
        tile(1, CT, BF16),
        tile(1, WIDE, F32),
        pltpu.VMEM((512, 9 * WIDE), BF16),
        pltpu.VMEM((2, 3, 3, 3, WIDE, CT), BF16),
        pltpu.VMEM((3, 512, CT), F32),
        pltpu.VMEM((8, TH, 2, 8, CS), BF16),
        pltpu.VMEM((512, CS), F32),
        tile(2, CS, F32),
        tile(2, CS, F32),
        tile(2, CS, F32),
        tile(1, CS, F32),
        tile(1, CS, F32),
        tile(1, CS, F32),
        tile(0, CS, F32),
        tile(0, CS, F32),
        tile(0, CS, F32),
        tile(1, CS, F32),
        tile(2, CS, F32),
        tile(2, CS, BF16),
        tile(2, CS, BF16),
        tile(3, CS, BF16),
        tile(4, CS, BF16),
        tile(4, CS, F32),
        tile(4, CS, F32),
        tile(3, CS, F32),
        tile(2, CS, F32),
        pltpu.VMEM((512, CS), BF16),
        pltpu.VMEM((512, CT), BF16),
        pltpu.VMEM((512, CT), F32),
        pltpu.VMEM((8, TH, 2, 8, CS), BF16),
        pltpu.VMEM((3, 3, 3, 4, CS), F32),
        pltpu.VMEM((4, CS, CS), BF16),
        pltpu.VMEM((CT, CS), BF16),
        dma((9,)),
        dma(()),
        dma(()),
        dma(()),
        dma(()),
        dma(()),
        dma(()),
        dma((7, 8)),
        dma((7, 8)),
    ]
    result = pl.pallas_call(
        kernel,
        out_shape=jax.ShapeDtypeStruct((2, 32, 8, CS), BF16),
        in_specs=[anywhere] * 6,
        out_specs=anywhere,
        scratch_shapes=scratch,
        compiler_params=pltpu.CompilerParams(
            collective_id=0, has_side_effects=True, vmem_limit_bytes=56 * 1024 * 1024
        ),
    )(tin, tw, sin.reshape(2, 32, 8, CS), dw.transpose(1, 2, 3, 0, 4), pw, proj.T)
    return result.reshape(2, 1, 256, CS)


def solution(mesh):
    rows = P("ta", ("ha", "wa"), None, None)
    return jax.shard_map(
        on_device,
        mesh=mesh,
        in_specs=(P("ta", "ha", "wa", None), P(), rows, P(), P(), P()),
        out_specs=rows,
        check_vma=False,
    )
```
